32 devices in a mesh: groups: 2 (over x), dap: 16 (over z, y, core).
Axes of the slice: x: 2, y: 2, z: 4, core: 2. Of those that a mesh axis runs over, the one named last changes fastest.
Arguments:
- pair_state: bfloat16 [128, 64, 128], P(('groups', 'dap')), parts along dimension 0, may hold values from -200 to 200
- cotangent: bfloat16 [128, 64, 128], P(('groups', 'dap')), parts along dimension 0, may hold values from -6 to 6
- pair_mask: int32 [128, 64], P(('groups', 'dap')), parts along dimension 0, may hold values 0 or 1
- token_count: int32 [2], P('groups'), parts along dimension 0, may hold values from 32 to 64
- norm_gain: float32 [128], replicated, may hold values from 0.1 to 1.9
- norm_shift: float32 [128], replicated, may hold values from -3 to 3
- w_edges: bfloat16 [128, 256], replicated, may hold values from -0.5 to 0.5
- w_gate: bfloat16 [128, 128], replicated, may hold values from -0.5 to 0.5
- edge_gain: float32 [64], replicated, may hold values from 0.1 to 1.9
- edge_shift: float32 [64], replicated, may hold values from -3 to 3
- w_out: bfloat16 [64, 128], replicated, may hold values from -0.75 to 0.75
- final_gain: float32 [128], replicated, may hold values from 0.1 to 1.9
- final_shift: float32 [128], replicated, may hold values from -3 to 3
- w_expand: bfloat16 [128, 1024], replicated, may hold values from -0.5 to 0.5
- w_contract: bfloat16 [512, 128], replicated, may hold values from -0.25 to 0.25
Outputs:
- grad_pair: bfloat16 [128, 64, 128], P(('groups', 'dap')), parts along dimension 0
- norm_grads: float32 [8, 128], P('groups'), parts along dimension 0
- edge_grads: float32 [4, 64], P('groups'), parts along dimension 0
The draws below stay inside these ranges and needn't reach their ends.
There are 2 independent parts, one for each index of `groups`. The reference program is written for one: setup_inputs(seed, part) draws one part's arguments, and reference() takes and returns one part's arrays. A program takes and returns all parts, laid end to end along the dimension named above; an argument that names none is the same for every part. Nothing has to cross between parts.
All inputs are finite; a program needn't handle non-finite values. No bound on the sum of `pair_mask` on one device may be relied on, other than what follows from the above.
Results may differ from the reference program's by a relative error of at most 0.012.
Values may be sent and summed in bfloat16 or wider, within the bound.
A program may use at most 192 MiB of HBM per device.

```python
import math
import jax
import jax.numpy as jnp
from jax import lax

PAIR_WIDTH = 128
EDGE_WIDTH = 64
TRANSITION_UNITS = 512
TOKENS = 64


def draw_pair_state(key, part):
    key = jax.random.fold_in(key, 11)
    key_base, key_cell, key_chan = jax.random.split(key, 3)
    cell_scale = jnp.exp(jax.random.uniform(key_cell, (TOKENS, TOKENS, 1), minval=0.0, maxval=math.log(10.0)))
    chan_scale = jnp.exp(jax.random.uniform(key_chan, (1, 1, PAIR_WIDTH), minval=math.log(0.5), maxval=math.log(5.0)))
    base = jnp.clip(jax.random.normal(key_base, (TOKENS, TOKENS, PAIR_WIDTH)), -4.0, 4.0)
    return (base * cell_scale * chan_scale).astype(jnp.bfloat16)


def with_ends(drawn, key, smallest, high):
    spot = [jax.random.randint(jax.random.fold_in(key, axis), (), 0, length) for axis, length in enumerate(drawn.shape)]
    main_axis = drawn.shape.index(max(drawn.shape))
    beside = spot[:main_axis] + [(spot[main_axis] + 1) % drawn.shape[main_axis]] + spot[main_axis + 1:]
    return drawn.at[tuple(spot)].set(smallest).at[tuple(beside)].set(high)


def levels(stream_key, extent, pieces, low, top_value):
    def one(axis_at, blocks):
        draws = jax.random.uniform(jax.random.fold_in(jax.random.fold_in(stream_key, 6), axis_at), (blocks,), jnp.float32, low / len(pieces), top_value / len(pieces))
        return jnp.repeat(jnp.exp(draws), extent[axis_at] // blocks).reshape((-1,) + (1,) * (len(extent) - axis_at - 1))

    loudness = one(*pieces[0])
    for cut in pieces[1:]:
        loudness = loudness * one(*cut)
    return loudness


def noise(stream_key, shape, scale, most, cuts=(), kind=jnp.bfloat16):
    values = jax.random.normal(stream_key, shape, jnp.float32) * scale
    if len(cuts) > 0:
        values = levels(stream_key, shape, cuts, -0.22, 0.18) * values
    return jnp.clip(values, min=-most, max=most).astype(kind)


def setup_inputs(seed: int = 0, part: int = 0) -> dict:
    seeds = jax.random.split(jax.random.key(seed), 16)
    part_keys = jax.random.split(jax.random.fold_in(seeds[15], part), 16)
    return {
        "pair_state": draw_pair_state(jax.random.fold_in(jax.random.fold_in(seeds[15], part), 71), part),
        "cotangent": noise(part_keys[1], (TOKENS, TOKENS, PAIR_WIDTH), 1.0, 6.0, ((0, 16),)),
        "pair_mask": with_ends((jax.random.randint(part_keys[2], (TOKENS, TOKENS), 0, 8) < 7).astype(jnp.int32), jax.random.fold_in(part_keys[2], 1), 0, 1),
        "token_count": jax.random.randint(part_keys[3], (1,), TOKENS // 2, TOKENS + 1).astype(jnp.int32),
        "norm_gain": jnp.clip(1.0 + 0.18 * jax.random.normal(seeds[4], (PAIR_WIDTH,), jnp.float32), 0.1, 1.9),
        "norm_shift": noise(seeds[5], (PAIR_WIDTH,), 0.5, 3.0, (), jnp.float32),
        "w_edges": noise(seeds[6], (PAIR_WIDTH, 4 * EDGE_WIDTH), PAIR_WIDTH ** -0.5, 0.5),
        "w_gate": noise(seeds[7], (PAIR_WIDTH, PAIR_WIDTH), PAIR_WIDTH ** -0.5, 0.5),
        "edge_gain": jnp.clip(1.0 + 0.18 * jax.random.normal(seeds[8], (EDGE_WIDTH,), jnp.float32), 0.1, 1.9),
        "edge_shift": noise(seeds[9], (EDGE_WIDTH,), 0.5, 3.0, (), jnp.float32),
        "w_out": noise(seeds[10], (EDGE_WIDTH, PAIR_WIDTH), EDGE_WIDTH ** -0.5, 0.75),
        "final_gain": jnp.clip(1.0 + 0.18 * jax.random.normal(seeds[11], (PAIR_WIDTH,), jnp.float32), 0.1, 1.9),
        "final_shift": noise(seeds[12], (PAIR_WIDTH,), 0.5, 3.0, (), jnp.float32),
        "w_expand": noise(seeds[13], (PAIR_WIDTH, 2 * TRANSITION_UNITS), PAIR_WIDTH ** -0.5, 0.5),
        "w_contract": noise(seeds[14], (TRANSITION_UNITS, PAIR_WIDTH), TRANSITION_UNITS ** -0.5, 0.25),
    }


epsilon = 1e-05

def layer_norm(values, norm_scale, norm_offset):
    centre = lax.optimization_barrier(jnp.mean(values, axis=-1, keepdims=True))
    centred = values - centre
    spread = lax.optimization_barrier(jnp.mean(centred * centred, axis=-1, keepdims=True))
    return centred * lax.rsqrt(spread + epsilon) * norm_scale + norm_offset

def project_edges(state, validity, scale_in, offset_in, w_edges, w_gate):
    normed = layer_norm(state.astype(jnp.float32), scale_in, offset_in).astype(jnp.bfloat16)
    channels = w_edges.shape[1] // 4
    mixed = jnp.dot(normed, w_edges, preferred_element_type=jnp.float32)
    weight_mask = validity[..., None]
    left_edges = jax.nn.sigmoid(mixed[..., :channels]) * mixed[..., channels:2 * channels] * weight_mask
    right_edges = jax.nn.sigmoid(mixed[..., 2 * channels:3 * channels]) * mixed[..., 3 * channels:] * weight_mask
    gating = jax.nn.sigmoid(jnp.dot(normed, w_gate, preferred_element_type=jnp.float32))
    return (left_edges.astype(jnp.bfloat16), right_edges.astype(jnp.bfloat16), gating.astype(jnp.bfloat16))

def finish_block(state, edges, gating, edge_scale, edge_offset, final_scale, final_offset, w_out, w_expand, w_contract):
    edge_normed = layer_norm(edges, edge_scale, edge_offset).astype(jnp.bfloat16)
    update = gating.astype(jnp.float32) * jnp.dot(edge_normed, w_out, preferred_element_type=jnp.float32)
    middle = (state.astype(jnp.float32) + update).astype(jnp.bfloat16).astype(jnp.float32)
    normed = layer_norm(middle, final_scale, final_offset).astype(jnp.bfloat16)
    expanded = jnp.dot(normed, w_expand, preferred_element_type=jnp.float32)
    hidden_units = w_contract.shape[0]
    activated = (jax.nn.silu(expanded[..., :hidden_units]) * expanded[..., hidden_units:]).astype(jnp.bfloat16)
    return middle + jnp.dot(activated, w_contract, preferred_element_type=jnp.float32)

def reference(pair_state, cotangent, pair_mask, token_count, norm_gain, norm_shift, w_edges, w_gate, edge_gain, edge_shift, w_out, final_gain, final_shift, w_expand, w_contract):
    live_count = token_count[0]
    positions = jnp.arange(TOKENS, dtype=jnp.int32)
    inside = (positions < live_count).astype(jnp.float32)
    validity = pair_mask.astype(jnp.float32) * inside[:, None] * inside[None, :]

    def project_whole(state_in, scale_in, offset_in):
        return project_edges(state_in, validity, scale_in, offset_in, w_edges, w_gate)
    outputs, project_back = jax.vjp(project_whole, pair_state, norm_gain, norm_shift)
    left_edges, right_edges, gating = lax.optimization_barrier(outputs)
    left_rows = left_edges.transpose(2, 0, 1).astype(jnp.float32)
    right_rows = right_edges.transpose(2, 0, 1).astype(jnp.float32)
    edges = jnp.einsum('cik,cjk->cij', left_rows, right_rows)

    def finish_whole(state_in, edges_in, gate_in, scale_a, offset_a, scale_b, offset_b):
        return finish_block(state_in, edges_in, gate_in, scale_a, offset_a, scale_b, offset_b, w_out, w_expand, w_contract)
    _, finish_back = jax.vjp(finish_whole, pair_state, edges.transpose(1, 2, 0), gating, edge_gain, edge_shift, final_gain, final_shift)
    grads = finish_back(cotangent.astype(jnp.float32))
    edge_round = lax.optimization_barrier(grads[1].transpose(2, 0, 1).astype(jnp.bfloat16)).astype(jnp.float32)
    left_grad = jnp.einsum('cij,cjk->cik', edge_round, right_rows).astype(jnp.bfloat16)
    right_grad = jnp.einsum('cij,cik->cjk', edge_round, left_rows).astype(jnp.bfloat16)
    cotangents = lax.optimization_barrier((left_grad.transpose(1, 2, 0), right_grad.transpose(1, 2, 0), grads[2]))
    early_grad, gain_grad, shift_grad = project_back(cotangents)
    summed = lax.optimization_barrier((early_grad, grads[0]))
    grad_pair = (summed[0].astype(jnp.float32) + summed[1].astype(jnp.float32)).astype(jnp.bfloat16)
    norm_grads = jnp.stack([gain_grad, shift_grad, grads[5], grads[6]]) / TOKENS
    edge_grads = jnp.stack([grads[3], grads[4]]) / TOKENS
    return (grad_pair, norm_grads, edge_grads)
```

```python
import functools

import jax
import jax.numpy as jnp
from jax import lax
from jax.experimental import pallas as pl
from jax.experimental.pallas import tpu as pltpu
from jax.sharding import PartitionSpec as P

epsilon = 1e-05
block_cols = 64


def layer_norm(values, norm_scale, norm_offset):
    centre = jnp.mean(values, axis=-1, keepdims=True)
    centred = values - centre
    spread = jnp.mean(centred * centred, axis=-1, keepdims=True)
    return centred * lax.rsqrt(spread + epsilon) * norm_scale + norm_offset


def project_edges(state, validity, scale_in, offset_in, w_edges, w_gate):
    normed = layer_norm(state.astype(jnp.float32), scale_in, offset_in).astype(jnp.bfloat16)
    channels = w_edges.shape[1] // 4
    mixed = jnp.dot(normed, w_edges, preferred_element_type=jnp.float32)
    weight_mask = validity[..., None]
    left_edges = (
        jax.nn.sigmoid(mixed[..., :channels]) * mixed[..., channels : 2 * channels] * weight_mask
    )
    right_edges = (
        jax.nn.sigmoid(mixed[..., 2 * channels : 3 * channels])
        * mixed[..., 3 * channels :]
        * weight_mask
    )
    gating = jax.nn.sigmoid(jnp.dot(normed, w_gate, preferred_element_type=jnp.float32))
    return (
        left_edges.astype(jnp.bfloat16),
        right_edges.astype(jnp.bfloat16),
        gating.astype(jnp.bfloat16),
    )


def finish_block(
    state,
    edges,
    gating,
    edge_scale,
    edge_offset,
    final_scale,
    final_offset,
    w_out,
    w_expand,
    w_contract,
):
    edge_normed = layer_norm(edges, edge_scale, edge_offset).astype(jnp.bfloat16)
    update = gating.astype(jnp.float32) * jnp.dot(
        edge_normed, w_out, preferred_element_type=jnp.float32
    )
    middle = (state.astype(jnp.float32) + update).astype(jnp.bfloat16).astype(jnp.float32)
    normed = layer_norm(middle, final_scale, final_offset).astype(jnp.bfloat16)
    expanded = jnp.dot(normed, w_expand, preferred_element_type=jnp.float32)
    hidden_units = w_contract.shape[0]
    activated = (jax.nn.silu(expanded[..., :hidden_units]) * expanded[..., hidden_units:]).astype(
        jnp.bfloat16
    )
    return middle + jnp.dot(activated, w_contract, preferred_element_type=jnp.float32)


def body(
    pair_state,
    cotangent,
    pair_mask,
    token_count,
    norm_gain,
    norm_shift,
    w_edges,
    w_gate,
    edge_gain,
    edge_shift,
    w_out,
    final_gain,
    final_shift,
    w_expand,
    w_contract,
):
    rows_dev = pair_state.shape[0]
    tokens_all = pair_state.shape[1]
    first_row = lax.axis_index("dap") * rows_dev
    row_ids = first_row + jnp.arange(rows_dev, dtype=jnp.int32)
    column_ids = jnp.arange(tokens_all, dtype=jnp.int32)
    live_count = token_count[0]
    validity = (
        pair_mask.astype(jnp.float32)
        * (row_ids < live_count).astype(jnp.float32)[:, None]
        * (column_ids < live_count).astype(jnp.float32)[None, :]
    )

    def project_local(state_in, scale_in, offset_in):
        return project_edges(state_in, validity, scale_in, offset_in, w_edges, w_gate)

    outputs, project_back = jax.vjp(project_local, pair_state, norm_gain, norm_shift)
    left_edges, right_edges, gating = lax.optimization_barrier(outputs)
    left_rows = left_edges.transpose(2, 0, 1)
    right_rows = right_edges.transpose(2, 0, 1)
    channels = left_rows.shape[0]

    def finish_local(state_in, edges_in, gate_in, scale_a, offset_a, scale_b, offset_b):
        return finish_block(
            state_in,
            edges_in,
            gate_in,
            scale_a,
            offset_a,
            scale_b,
            offset_b,
            w_out,
            w_expand,
            w_contract,
        )

    def absorb_block(carry_in, piece_rows, offset_at):
        left_grad, edge_grads_all, state_grad, gate_grad, norm_sums = carry_in
        width_now = piece_rows.shape[1]
        edges = jnp.einsum(
            "cik,cjk->cij", left_rows, piece_rows, preferred_element_type=jnp.float32
        )
        state_part = lax.dynamic_slice_in_dim(pair_state, offset_at, width_now, 1)
        gate_part = lax.dynamic_slice_in_dim(gating, offset_at, width_now, 1)
        cotan_part = lax.dynamic_slice_in_dim(cotangent, offset_at, width_now, 1)
        _, finish_back = jax.vjp(
            finish_local,
            state_part,
            edges.transpose(1, 2, 0),
            gate_part,
            edge_gain,
            edge_shift,
            final_gain,
            final_shift,
        )
        grads = finish_back(cotan_part.astype(jnp.float32))
        edge_round = grads[1].transpose(2, 0, 1).astype(jnp.bfloat16)
        left_grad = left_grad + jnp.einsum(
            "cij,cjk->cik", edge_round, piece_rows, preferred_element_type=jnp.float32
        )
        edge_grads_all = lax.dynamic_update_slice_in_dim(edge_grads_all, edge_round, offset_at, 2)
        state_grad = lax.dynamic_update_slice_in_dim(state_grad, grads[0], offset_at, 1)
        gate_grad = lax.dynamic_update_slice_in_dim(gate_grad, grads[2], offset_at, 1)
        norm_sums = (
            norm_sums[0] + grads[3],
            norm_sums[1] + grads[4],
            norm_sums[2] + grads[5],
            norm_sums[3] + grads[6],
        )
        return (left_grad, edge_grads_all, state_grad, gate_grad, norm_sums)

    def absorb(carry_in, piece_rows, offset_at):
        width_now = piece_rows.shape[1]
        if width_now > block_cols and width_now % block_cols == 0:

            def step_block(index_at, carry_now):
                begin = index_at * block_cols
                part_rows = lax.dynamic_slice_in_dim(piece_rows, begin, block_cols, 1)
                return absorb_block(carry_now, part_rows, offset_at + begin)

            return lax.fori_loop(0, width_now // block_cols, step_block, carry_in)
        return absorb_block(carry_in, piece_rows, offset_at)

    start_carry = (
        jnp.zeros((channels, rows_dev, tokens_all), jnp.float32),
        jnp.zeros((channels, rows_dev, tokens_all), jnp.bfloat16),
        jnp.zeros(pair_state.shape, jnp.bfloat16),
        jnp.zeros(gating.shape, jnp.bfloat16),
        (
            jnp.zeros(edge_gain.shape, jnp.float32),
            jnp.zeros(edge_shift.shape, jnp.float32),
            jnp.zeros(final_gain.shape, jnp.float32),
            jnp.zeros(final_shift.shape, jnp.float32),
        ),
    )
    left_sum, edge_grads_all, late_grad, gate_grad, norm_sums = absorb(
        start_carry, lax.all_gather(right_rows, "dap", axis=1, tiled=True), jnp.int32(0)
    )
    left_grad = left_sum.astype(jnp.bfloat16)
    columns = lax.all_to_all(edge_grads_all, "dap", split_axis=2, concat_axis=1, tiled=True)
    piece_rows = lax.all_gather(left_rows, "dap", axis=1, tiled=True)
    width_now = piece_rows.shape[1]
    right_sum = jnp.einsum("cij,cik->cjk", columns, piece_rows, preferred_element_type=jnp.float32)
    right_grad = right_sum.astype(jnp.bfloat16)
    cotangents = lax.optimization_barrier(
        (left_grad.transpose(1, 2, 0), right_grad.transpose(1, 2, 0), gate_grad)
    )
    early_grad, gain_grad, shift_grad = project_back(cotangents)
    summed = lax.optimization_barrier((early_grad, late_grad))
    grad_pair = (summed[0].astype(jnp.float32) + summed[1].astype(jnp.float32)).astype(jnp.bfloat16)
    pair_terms = jnp.stack([gain_grad, shift_grad, norm_sums[2], norm_sums[3]])
    edge_terms = jnp.stack([norm_sums[0], norm_sums[1]])
    pair_totals, edge_totals = lax.psum((pair_terms, edge_terms), "dap")
    return (grad_pair, pair_totals / tokens_all, edge_totals / tokens_all)

nn_dims = (((1,), (0,)), ((), ()))
nt_dims = (((1,), (1,)), ((), ()))
tn_dims = (((0,), (0,)), ((), ()))
f32 = jnp.float32
bf16 = jnp.bfloat16


def mul(a, b, dims):
    return lax.dot_general(a, b, dims, preferred_element_type=f32)


def sigmoid(x):
    return 0.5 * jnp.tanh(0.5 * x) + 0.5


def iota(shape, axis):
    return lax.broadcasted_iota(jnp.int32, shape, axis)


def low_half(rows):
    return iota((rows, 128), 1) < 64


def pack(x):
    low, high = x[:32], x[32:]
    first = low_half(32)
    pieces = []
    for half in range(2):
        a, b = low[:, half * 128 : half * 128 + 128], high[:, half * 128 : half * 128 + 128]
        pieces.append(jnp.where(first, a, pltpu.roll(b, 64, 1)))
        pieces.append(jnp.where(first, pltpu.roll(a, 64, 1), b))
    return jnp.concatenate(pieces, axis=0)


def unpack(x):
    first = low_half(32)
    lows, highs = [], []
    for half in range(2):
        a, b = x[half * 64 : half * 64 + 32], x[half * 64 + 32 : half * 64 + 64]
        lows.append(jnp.where(first, a, pltpu.roll(b, 64, 1)))
        highs.append(jnp.where(first, pltpu.roll(a, 64, 1), b))
    return jnp.concatenate(
        [jnp.concatenate(lows, axis=1), jnp.concatenate(highs, axis=1)], axis=0
    )


def one_hot(hit):
    return jnp.where(hit, 1.0, 0.0).astype(bf16)


def channel_sum(x):
    total = jnp.sum(x, axis=0)
    total = total + pltpu.roll(total, 4, 0)
    return total + pltpu.roll(total, 64, 1)


def fused_kernel(
    n,
    count_ref,
    state_ref,
    cot_ref,
    mask_ref,
    gain1_ref,
    shift1_ref,
    we_ref,
    wg_ref,
    gain_e_ref,
    shift_e_ref,
    wo_ref,
    gain2_ref,
    shift2_ref,
    wx_ref,
    wc_ref,
    out_ref,
    norm_ref,
    edge_ref,
    s1,
    r1,
    s2,
    r2,
    s3,
    r3,
    s4,
    r4,
    s5,
    r5,
    dact_ref,
    send_sem,
    recv_sem,
):
    me = lax.axis_index("dap")
    group = lax.axis_index("groups")
    cells = state_ref.shape[0] * state_ref.shape[1]
    tokens = state_ref.shape[1]

    barrier = pltpu.get_barrier_semaphore()

    def greet(step, carry):
        peer = lax.rem(me + step, n)
        pl.semaphore_signal(
            barrier, inc=1, device_id=(group, peer), device_id_type=pl.DeviceIdType.MESH
        )
        return carry

    lax.fori_loop(1, n, greet, 0)

    def scatter(phase, src, dst, same):
        def send(step, carry):
            peer = lax.rem(me + step, n)
            pltpu.make_async_remote_copy(
                src_ref=src if same else src.at[peer],
                dst_ref=dst.at[me],
                send_sem=send_sem.at[phase],
                recv_sem=recv_sem.at[phase],
                device_id=(group, peer),
                device_id_type=pl.DeviceIdType.MESH,
            ).start()
            return carry

        lax.fori_loop(1, n, send, 0)

    def arrive(phase, dst):
        part = dst.at[pl.ds(0, n - 1)]
        pltpu.make_async_copy(part, part, recv_sem.at[phase]).wait()

    def sent(phase, dst):
        part = dst.at[pl.ds(0, n - 1)]
        pltpu.make_async_copy(part, part, send_sem.at[phase]).wait()

    state = state_ref[...].reshape(cells, 128).astype(f32)
    gain1 = gain1_ref[...]
    centred = state - jnp.mean(state, axis=1, keepdims=True)
    rstd1 = lax.rsqrt(jnp.mean(centred * centred, axis=1, keepdims=True) + epsilon)
    hat1 = centred * rstd1
    normed = (hat1 * gain1 + shift1_ref[...]).astype(bf16)
    we_t = we_ref[...].T
    mixed = mul(we_t, normed, nt_dims)
    count = count_ref[0]
    mask = mask_ref[...].astype(f32)
    mask = jnp.concatenate([mask[i : i + 1] for i in range(4)], axis=1)
    cell = iota((1, cells), 1)
    live = (cell % tokens < count) & (me * 4 + cell // tokens < count)
    valid = jnp.where(live, mask, 0.0)
    sig_l, val_l = sigmoid(mixed[:64]), mixed[64:128]
    sig_r, val_r = sigmoid(mixed[128:192]), mixed[192:]
    left = pack(sig_l * val_l * valid).astype(bf16)
    right = pack(sig_r * val_r * valid).astype(bf16)
    row, col = iota((128, 128), 0), iota((128, 128), 1)
    to_owner = one_hot(col == (row % 4) * 32 + (row // 8) * 2 + (row // 4) % 2)
    from_owner = one_hot(row == (col % 4) * 32 + (col // 8) * 2 + (col // 4) % 2)
    both = mul(to_owner, jnp.concatenate([left, right], axis=1), nn_dims)
    both = jnp.concatenate(
        [both[:, :128].reshape(n, 8, 128), both[:, 128:].reshape(n, 8, 128)], axis=1
    ).astype(bf16)
    s1[...] = both
    r1[me] = s1[me]
    pl.semaphore_wait(barrier, n - 1)
    scatter(0, s1, r1, False)

    gating = sigmoid(mul(normed, wg_ref[...], nn_dims)).astype(bf16).astype(f32)
    cot = cot_ref[...].reshape(cells, 128)
    dact_ref[...] = mul(cot, wc_ref[...], nt_dims).astype(bf16)
    lane64 = iota((128, 64), 1)
    row64 = iota((128, 64), 0) // 4
    first = low_half(128)

    def spread(vector):
        low = jnp.sum(jnp.where(lane64 == row64, vector, 0.0), axis=1, keepdims=True)
        high = jnp.sum(jnp.where(lane64 == row64 + 32, vector, 0.0), axis=1, keepdims=True)
        return jnp.where(first, low, high).reshape(n, 8, 128)

    gain_e, shift_e = spread(gain_e_ref[...]), spread(shift_e_ref[...])
    by_pair = one_hot(col == ((row % 64) // 4) * 8 + (row // 64) * 4 + row % 4)
    pair_rows = one_hot(row == ((col % 64) // 4) * 8 + (col // 64) * 4 + col % 4)
    even = (iota((128, 128), 0) // 4) % 2 == 0

    arrive(0, r1)
    got = r1[...].astype(f32)
    left_all = got[:, :8].reshape(128, 128)
    right_all = mul(by_pair, got[:, 8:].reshape(128, 128).astype(bf16), nn_dims)
    first64 = low_half(64)

    def diagonal(x):
        return jnp.concatenate([jnp.where(first64, x, 0.0), jnp.where(first64, 0.0, x)], axis=0)

    diag0 = diagonal(right_all[:64]).astype(bf16)
    diag1 = diagonal(right_all[64:]).astype(bf16)

    def by_parity(x):
        return jnp.where(even, x, 0.0).astype(bf16), jnp.where(even, 0.0, x).astype(bf16)

    left0, left1 = by_parity(left_all)
    edges = mul(left0, diag0, nt_dims) + mul(left1, diag1, nt_dims)
    s2[...] = edges.reshape(n, 8, 128)
    r2[me] = s2[me]
    scatter(1, s2, r2, False)
    left_bf = left_all.astype(bf16)
    arrive(1, r2)

    edges_in = r2[...]
    inv_c = 1.0 / 64
    centred_e = edges_in - channel_sum(edges_in) * inv_c
    rstd_e = lax.rsqrt(channel_sum(centred_e * centred_e) * inv_c + epsilon)
    hat_e = centred_e * rstd_e
    edge_normed = (hat_e * gain_e + shift_e).reshape(128, 128).astype(bf16)
    edge_normed = unpack(mul(from_owner, edge_normed, nn_dims)).astype(bf16)
    update = mul(edge_normed, wo_ref[...], tn_dims)
    middle = (state + gating * update).astype(bf16).astype(f32)
    centred2 = middle - jnp.mean(middle, axis=1, keepdims=True)
    rstd2 = lax.rsqrt(jnp.mean(centred2 * centred2, axis=1, keepdims=True) + epsilon)
    hat2 = centred2 * rstd2
    gain2 = gain2_ref[...]
    normed2 = (hat2 * gain2 + shift2_ref[...]).astype(bf16)
    units = wc_ref.shape[0]
    dnormed2 = jnp.zeros((cells, 128), f32)
    for begin in range(0, units, 256):
        w_swish = wx_ref[:, begin : begin + 256]
        w_linear = wx_ref[:, units + begin : units + begin + 256]
        swish_in = mul(normed2, w_swish, nn_dims)
        linear = mul(normed2, w_linear, nn_dims)
        dact = dact_ref[:, begin : begin + 256].astype(f32)
        sig = sigmoid(swish_in)
        silu = swish_in * sig
        dlinear = (dact * silu).astype(bf16)
        dswish = (dact * linear * (sig + silu * (1.0 - sig))).astype(bf16)
        dnormed2 = dnormed2 + mul(dswish, w_swish, nt_dims) + mul(dlinear, w_linear, nt_dims)
    dnormed2 = dnormed2.astype(bf16).astype(f32)
    dhat2 = dnormed2 * gain2
    dmiddle = rstd2 * (
        dhat2
        - jnp.mean(dhat2, axis=1, keepdims=True)
        - hat2 * jnp.mean(dhat2 * hat2, axis=1, keepdims=True)
    )
    late = (cot.astype(f32) + dmiddle).astype(bf16).astype(f32)
    dedge = mul(wo_ref[...], (late * gating).astype(bf16), nt_dims)
    dedge = pack(dedge).astype(bf16)
    dedge = mul(to_owner, dedge, nn_dims).reshape(n, 8, 128)
    dhat_e = dedge * gain_e
    edge_raw = rstd_e * (
        dhat_e - channel_sum(dhat_e) * inv_c - hat_e * (channel_sum(dhat_e * hat_e) * inv_c)
    )
    s3[...] = edge_raw.astype(bf16).astype(f32)
    r3[me] = s3[me]
    scatter(2, s3, r3, False)

    gate_grad = (late * update).astype(bf16).astype(f32)
    dgate = (gate_grad * gating * (1.0 - gating)).astype(bf16)
    dnormed = mul(dgate, wg_ref[...], nt_dims)
    gain2_sum = jnp.sum(dnormed2 * hat2, axis=0, keepdims=True)
    shift2_sum = jnp.sum(dnormed2, axis=0, keepdims=True)

    def collect(x):
        x = x.reshape(128, 128)
        low = jnp.sum(jnp.where(first, x, 0.0), axis=1, keepdims=True)
        high = jnp.sum(jnp.where(first, 0.0, x), axis=1, keepdims=True)
        spot = row // 4
        return jnp.sum(
            jnp.where(col == spot, low, 0.0) + jnp.where(col == spot + 32, high, 0.0),
            axis=0,
            keepdims=True,
        )

    gain_e_sum = collect(dedge * hat_e)
    shift_e_sum = collect(dedge)
    dsig_l = val_l * sig_l * (1.0 - sig_l) * valid
    dsig_r = val_r * sig_r * (1.0 - sig_r) * valid
    dval_l, dval_r = sig_l * valid, sig_r * valid

    arrive(2, r3)
    edge_round = r3[...].reshape(128, 128)
    round0, round1 = by_parity(edge_round)
    left_grad = mul(round0, diag0, nn_dims) + mul(round1, diag1, nn_dims)
    cross0 = mul(round0, left_bf, tn_dims)
    cross1 = mul(round1, left_bf, tn_dims)
    right_grad = jnp.concatenate(
        [
            jnp.where(first64, cross0[:64], cross0[64:]),
            jnp.where(first64, cross1[:64], cross1[64:]),
        ],
        axis=0,
    ).astype(bf16)
    right_grad = mul(pair_rows, right_grad, nn_dims)
    s4[...] = jnp.concatenate(
        [left_grad.reshape(n, 8, 128), right_grad.reshape(n, 8, 128)], axis=1
    ).astype(bf16)
    r4[me] = s4[me]
    scatter(3, s4, r4, False)
    arrive(3, r4)

    grads = r4[...].astype(f32)
    grads = jnp.concatenate(
        [grads[:, :8].reshape(128, 128), grads[:, 8:].reshape(128, 128)], axis=1
    ).astype(bf16)
    grads = mul(from_owner, grads, nn_dims)
    dleft, dright = unpack(grads[:, :128]), unpack(grads[:, 128:])
    dmixed = jnp.concatenate(
        [dleft * dsig_l, dleft * dval_l, dright * dsig_r, dright * dval_r], axis=0
    ).astype(bf16)
    dnormed = (dnormed + mul(dmixed, we_t, tn_dims)).astype(bf16).astype(f32)
    gain1_sum = jnp.sum(dnormed * hat1, axis=0, keepdims=True)
    shift1_sum = jnp.sum(dnormed, axis=0, keepdims=True)
    blank = jnp.zeros((2, 128), f32)
    s5[...] = jnp.concatenate(
        [gain1_sum, shift1_sum, gain2_sum, shift2_sum, gain_e_sum, shift_e_sum, blank], axis=0
    )
    r5[me] = s5[...]
    scatter(4, s5, r5, True)
    dhat1 = dnormed * gain1
    early = rstd1 * (
        dhat1
        - jnp.mean(dhat1, axis=1, keepdims=True)
        - hat1 * jnp.mean(dhat1 * hat1, axis=1, keepdims=True)
    )
    early = early.astype(bf16).astype(f32)
    out_ref[...] = (early + late).astype(bf16).reshape(out_ref.shape)
    arrive(4, r5)
    sums = jnp.sum(r5[...], axis=0) * (1.0 / tokens)
    norm_ref[...] = sums[:4]
    edge_ref[...] = sums[4:6, :64]
    for phase, buffer in enumerate((r1, r2, r3, r4, r5)):
        sent(phase, buffer)


def fused_body(n, *args):
    (
        pair_state,
        cotangent,
        pair_mask,
        token_count,
        norm_gain,
        norm_shift,
        w_edges,
        w_gate,
        edge_gain,
        edge_shift,
        w_out,
        final_gain,
        final_shift,
        w_expand,
        w_contract,
    ) = args
    vmem = pl.BlockSpec(memory_space=pltpu.VMEM)
    cells = pair_state.shape[0] * pair_state.shape[1]
    tile = pltpu.VMEM((n, 8, 128), f32)
    pair = pltpu.VMEM((n, 16, 128), bf16)
    return pl.pallas_call(
        functools.partial(fused_kernel, n),
        out_shape=(
            jax.ShapeDtypeStruct(pair_state.shape, bf16),
            jax.ShapeDtypeStruct((4, 128), f32),
            jax.ShapeDtypeStruct((2, 64), f32),
        ),
        in_specs=[pl.BlockSpec(memory_space=pltpu.SMEM)] + [vmem] * 14,
        out_specs=(vmem, vmem, vmem),
        scratch_shapes=[
            pair,
            pair,
            tile,
            tile,
            tile,
            tile,
            pair,
            pair,
            pltpu.VMEM((8, 128), f32),
            tile,
            pltpu.VMEM((cells, w_contract.shape[0]), bf16),
            pltpu.SemaphoreType.DMA((5,)),
            pltpu.SemaphoreType.DMA((5,)),
        ],
        compiler_params=pltpu.CompilerParams(
            collective_id=0, has_side_effects=True, vmem_limit_bytes=32 * 1024 * 1024
        ),
    )(
        token_count,
        pair_state,
        cotangent,
        pair_mask,
        norm_gain.reshape(1, -1),
        norm_shift.reshape(1, -1),
        w_edges,
        w_gate,
        edge_gain.reshape(1, -1),
        edge_shift.reshape(1, -1),
        w_out,
        final_gain.reshape(1, -1),
        final_shift.reshape(1, -1),
        w_expand,
        w_contract,
    )


def pick_body(n):
    def chosen(*args):
        rows, tokens, _ = args[0].shape
        if (n, rows, tokens) == (16, 4, 64):
            return fused_body(n, *args)
        return body(*args)

    return chosen


def solution(mesh):
    in_specs = (
        P(("groups", "dap"), None, None),
        P(("groups", "dap"), None, None),
        P(("groups", "dap"), None),
        P("groups"),
        P(),
        P(),
        P(),
        P(),
        P(),
        P(),
        P(),
        P(),
        P(),
        P(),
        P(),
    )
    out_specs = (P(("groups", "dap"), None, None), P("groups", None), P("groups", None))
    chosen = pick_body(mesh.shape["dap"])
    return jax.shard_map(chosen, mesh=mesh, in_specs=in_specs, out_specs=out_specs, check_vma=False)
```

```python
import functools

import jax
import jax.numpy as jnp
from jax import lax
from jax.experimental import pallas as pl
from jax.experimental.pallas import tpu as pltpu
from jax.sharding import PartitionSpec as P

epsilon = 1e-05
block_cols = 64


def layer_norm(values, norm_scale, norm_offset):
    centre = jnp.mean(values, axis=-1, keepdims=True)
    centred = values - centre
    spread = jnp.mean(centred * centred, axis=-1, keepdims=True)
    return centred * lax.rsqrt(spread + epsilon) * norm_scale + norm_offset


def project_edges(state, validity, scale_in, offset_in, w_edges, w_gate):
    normed = layer_norm(state.astype(jnp.float32), scale_in, offset_in).astype(jnp.bfloat16)
    channels = w_edges.shape[1] // 4
    mixed = jnp.dot(normed, w_edges, preferred_element_type=jnp.float32)
    weight_mask = validity[..., None]
    left_edges = (
        jax.nn.sigmoid(mixed[..., :channels]) * mixed[..., channels : 2 * channels] * weight_mask
    )
    right_edges = (
        jax.nn.sigmoid(mixed[..., 2 * channels : 3 * channels])
        * mixed[..., 3 * channels :]
        * weight_mask
    )
    gating = jax.nn.sigmoid(jnp.dot(normed, w_gate, preferred_element_type=jnp.float32))
    return (
        left_edges.astype(jnp.bfloat16),
        right_edges.astype(jnp.bfloat16),
        gating.astype(jnp.bfloat16),
    )


def finish_block(
    state,
    edges,
    gating,
    edge_scale,
    edge_offset,
    final_scale,
    final_offset,
    w_out,
    w_expand,
    w_contract,
):
    edge_normed = layer_norm(edges, edge_scale, edge_offset).astype(jnp.bfloat16)
    update = gating.astype(jnp.float32) * jnp.dot(
        edge_normed, w_out, preferred_element_type=jnp.float32
    )
    middle = (state.astype(jnp.float32) + update).astype(jnp.bfloat16).astype(jnp.float32)
    normed = layer_norm(middle, final_scale, final_offset).astype(jnp.bfloat16)
    expanded = jnp.dot(normed, w_expand, preferred_element_type=jnp.float32)
    hidden_units = w_contract.shape[0]
    activated = (jax.nn.silu(expanded[..., :hidden_units]) * expanded[..., hidden_units:]).astype(
        jnp.bfloat16
    )
    return middle + jnp.dot(activated, w_contract, preferred_element_type=jnp.float32)


def body(
    pair_state,
    cotangent,
    pair_mask,
    token_count,
    norm_gain,
    norm_shift,
    w_edges,
    w_gate,
    edge_gain,
    edge_shift,
    w_out,
    final_gain,
    final_shift,
    w_expand,
    w_contract,
):
    rows_dev = pair_state.shape[0]
    tokens_all = pair_state.shape[1]
    first_row = lax.axis_index("dap") * rows_dev
    row_ids = first_row + jnp.arange(rows_dev, dtype=jnp.int32)
    column_ids = jnp.arange(tokens_all, dtype=jnp.int32)
    live_count = token_count[0]
    validity = (
        pair_mask.astype(jnp.float32)
        * (row_ids < live_count).astype(jnp.float32)[:, None]
        * (column_ids < live_count).astype(jnp.float32)[None, :]
    )

    def project_local(state_in, scale_in, offset_in):
        return project_edges(state_in, validity, scale_in, offset_in, w_edges, w_gate)

    outputs, project_back = jax.vjp(project_local, pair_state, norm_gain, norm_shift)
    left_edges, right_edges, gating = lax.optimization_barrier(outputs)
    left_rows = left_edges.transpose(2, 0, 1)
    right_rows = right_edges.transpose(2, 0, 1)
    channels = left_rows.shape[0]

    def finish_local(state_in, edges_in, gate_in, scale_a, offset_a, scale_b, offset_b):
        return finish_block(
            state_in,
            edges_in,
            gate_in,
            scale_a,
            offset_a,
            scale_b,
            offset_b,
            w_out,
            w_expand,
            w_contract,
        )

    def absorb_block(carry_in, piece_rows, offset_at):
        left_grad, edge_grads_all, state_grad, gate_grad, norm_sums = carry_in
        width_now = piece_rows.shape[1]
        edges = jnp.einsum(
            "cik,cjk->cij", left_rows, piece_rows, preferred_element_type=jnp.float32
        )
        state_part = lax.dynamic_slice_in_dim(pair_state, offset_at, width_now, 1)
        gate_part = lax.dynamic_slice_in_dim(gating, offset_at, width_now, 1)
        cotan_part = lax.dynamic_slice_in_dim(cotangent, offset_at, width_now, 1)
        _, finish_back = jax.vjp(
            finish_local,
            state_part,
            edges.transpose(1, 2, 0),
            gate_part,
            edge_gain,
            edge_shift,
            final_gain,
            final_shift,
        )
        grads = finish_back(cotan_part.astype(jnp.float32))
        edge_round = grads[1].transpose(2, 0, 1).astype(jnp.bfloat16)
        left_grad = left_grad + jnp.einsum(
            "cij,cjk->cik", edge_round, piece_rows, preferred_element_type=jnp.float32
        )
        edge_grads_all = lax.dynamic_update_slice_in_dim(edge_grads_all, edge_round, offset_at, 2)
        state_grad = lax.dynamic_update_slice_in_dim(state_grad, grads[0], offset_at, 1)
        gate_grad = lax.dynamic_update_slice_in_dim(gate_grad, grads[2], offset_at, 1)
        norm_sums = (
            norm_sums[0] + grads[3],
            norm_sums[1] + grads[4],
            norm_sums[2] + grads[5],
            norm_sums[3] + grads[6],
        )
        return (left_grad, edge_grads_all, state_grad, gate_grad, norm_sums)

    def absorb(carry_in, piece_rows, offset_at):
        width_now = piece_rows.shape[1]
        if width_now > block_cols and width_now % block_cols == 0:

            def step_block(index_at, carry_now):
                begin = index_at * block_cols
                part_rows = lax.dynamic_slice_in_dim(piece_rows, begin, block_cols, 1)
                return absorb_block(carry_now, part_rows, offset_at + begin)

            return lax.fori_loop(0, width_now // block_cols, step_block, carry_in)
        return absorb_block(carry_in, piece_rows, offset_at)

    start_carry = (
        jnp.zeros((channels, rows_dev, tokens_all), jnp.float32),
        jnp.zeros((channels, rows_dev, tokens_all), jnp.bfloat16),
        jnp.zeros(pair_state.shape, jnp.bfloat16),
        jnp.zeros(gating.shape, jnp.bfloat16),
        (
            jnp.zeros(edge_gain.shape, jnp.float32),
            jnp.zeros(edge_shift.shape, jnp.float32),
            jnp.zeros(final_gain.shape, jnp.float32),
            jnp.zeros(final_shift.shape, jnp.float32),
        ),
    )
    left_sum, edge_grads_all, late_grad, gate_grad, norm_sums = absorb(
        start_carry, lax.all_gather(right_rows, "dap", axis=1, tiled=True), jnp.int32(0)
    )
    left_grad = left_sum.astype(jnp.bfloat16)
    columns = lax.all_to_all(edge_grads_all, "dap", split_axis=2, concat_axis=1, tiled=True)
    piece_rows = lax.all_gather(left_rows, "dap", axis=1, tiled=True)
    width_now = piece_rows.shape[1]
    right_sum = jnp.einsum("cij,cik->cjk", columns, piece_rows, preferred_element_type=jnp.float32)
    right_grad = right_sum.astype(jnp.bfloat16)
    cotangents = lax.optimization_barrier(
        (left_grad.transpose(1, 2, 0), right_grad.transpose(1, 2, 0), gate_grad)
    )
    early_grad, gain_grad, shift_grad = project_back(cotangents)
    summed = lax.optimization_barrier((early_grad, late_grad))
    grad_pair = (summed[0].astype(jnp.float32) + summed[1].astype(jnp.float32)).astype(jnp.bfloat16)
    pair_terms = jnp.stack([gain_grad, shift_grad, norm_sums[2], norm_sums[3]])
    edge_terms = jnp.stack([norm_sums[0], norm_sums[1]])
    pair_totals, edge_totals = lax.psum((pair_terms, edge_terms), "dap")
    return (grad_pair, pair_totals / tokens_all, edge_totals / tokens_all)

nn_dims = (((1,), (0,)), ((), ()))
nt_dims = (((1,), (1,)), ((), ()))
tn_dims = (((0,), (0,)), ((), ()))
f32 = jnp.float32
bf16 = jnp.bfloat16


def mul(a, b, dims):
    return lax.dot_general(a, b, dims, preferred_element_type=f32)


def sigmoid(x):
    return 0.5 * jnp.tanh(0.5 * x) + 0.5


def iota(shape, axis):
    return lax.broadcasted_iota(jnp.int32, shape, axis)


def low_half(rows):
    return iota((rows, 128), 1) < 64


def pack(x):
    low, high = x[:32], x[32:]
    first = low_half(32)
    pieces = []
    for half in range(2):
        a, b = low[:, half * 128 : half * 128 + 128], high[:, half * 128 : half * 128 + 128]
        pieces.append(jnp.where(first, a, pltpu.roll(b, 64, 1)))
        pieces.append(jnp.where(first, pltpu.roll(a, 64, 1), b))
    return jnp.concatenate(pieces, axis=0)


def unpack(x):
    first = low_half(32)
    lows, highs = [], []
    for half in range(2):
        a, b = x[half * 64 : half * 64 + 32], x[half * 64 + 32 : half * 64 + 64]
        lows.append(jnp.where(first, a, pltpu.roll(b, 64, 1)))
        highs.append(jnp.where(first, pltpu.roll(a, 64, 1), b))
    return jnp.concatenate(
        [jnp.concatenate(lows, axis=1), jnp.concatenate(highs, axis=1)], axis=0
    )


def one_hot(hit):
    return jnp.where(hit, 1.0, 0.0).astype(bf16)


def channel_sum(x):
    total = jnp.sum(x, axis=0)
    total = total + pltpu.roll(total, 4, 0)
    return total + pltpu.roll(total, 64, 1)


names = (
    "state",
    "we",
    "gain1",
    "shift1",
    "mask",
    "real",
    "wg",
    "cot",
    "wc",
    "gain_e",
    "shift_e",
    "wo",
    "gain2",
    "shift2",
    "wx",
)


def fused_kernel(n, *refs):
    count = len(names)
    sources, refs = refs[:count], refs[count:]
    out_ref, norm_ref, edge_ref, *held = refs[: 3 + count]
    s1, r1, s2, r2, s3, r3, s4, r4, s5, r5, dact_ref, send_sem, recv_sem, load_sem = refs[3 + count :]
    me = lax.axis_index("dap")
    group = lax.axis_index("groups")
    loads = {
        name: pltpu.make_async_copy(sources[at], held[at], load_sem.at[at])
        for at, name in enumerate(names)
    }
    for name in names:
        loads[name].start()

    def load(name):
        loads[name].wait()
        return held[names.index(name)]

    rows, tokens = sources[0].shape[:2]
    cells = rows * tokens

    barrier = pltpu.get_barrier_semaphore()

    high, y, core = me // 8, (me // 2) % 2, me % 2
    z = me // 4
    peers = []
    for far in (3 - 3 * high, 2 - high, 1 - z + 4 * high):
        for side in (1 - y, y):
            peers += [far * 4 + side * 2 + 1 - core, far * 4 + side * 2 + core]
    peers += [z * 4 + (1 - y) * 2 + 1 - core, z * 4 + (1 - y) * 2 + core, z * 4 + y * 2 + 1 - core]

    for peer in peers:
        pl.semaphore_signal(
            barrier, inc=1, device_id=(group, peer), device_id_type=pl.DeviceIdType.MESH
        )

    def scatter(phase, src, dst, same):
        for peer in peers:
            pltpu.make_async_remote_copy(
                src_ref=src if same else src.at[peer],
                dst_ref=dst.at[me],
                send_sem=send_sem.at[phase],
                recv_sem=recv_sem.at[phase],
                device_id=(group, peer),
                device_id_type=pl.DeviceIdType.MESH,
            ).start()

    def arrive(phase, dst):
        part = dst.at[pl.ds(0, n - 1)]
        pltpu.make_async_copy(part, part, recv_sem.at[phase]).wait()

    def sent(phase, dst):
        part = dst.at[pl.ds(0, n - 1)]
        pltpu.make_async_copy(part, part, send_sem.at[phase]).wait()

    state = load("state")[...].reshape(cells, 128).astype(f32)
    gain1 = load("gain1")[...]
    centred = state - jnp.mean(state, axis=1, keepdims=True)
    rstd1 = lax.rsqrt(jnp.mean(centred * centred, axis=1, keepdims=True) + epsilon)
    hat1 = centred * rstd1
    normed = (hat1 * gain1 + load("shift1")[...]).astype(bf16)
    we_t = load("we")[...].T
    mixed = mul(we_t, normed, nt_dims)
    real = load("real")[...]
    mask = load("mask")[...].astype(f32)
    mask = jnp.concatenate([mask[i : i + 1] for i in range(rows)], axis=1)
    cell = iota((1, cells), 1)
    live = (cell % tokens < real) & (me * rows + cell // tokens < real)
    valid = jnp.where(live, mask, 0.0)
    sig_l, val_l = sigmoid(mixed[:64]), mixed[64:128]
    sig_r, val_r = sigmoid(mixed[128:192]), mixed[192:]
    left = pack(sig_l * val_l * valid).astype(bf16)
    right = pack(sig_r * val_r * valid).astype(bf16)
    row, col = iota((128, 128), 0), iota((128, 128), 1)
    to_owner = one_hot(col == (row % 4) * 32 + (row // 8) * 2 + (row // 4) % 2)
    from_owner = one_hot(row == (col % 4) * 32 + (col // 8) * 2 + (col // 4) % 2)
    both = mul(to_owner, jnp.concatenate([left, right], axis=1), nn_dims)
    both = jnp.concatenate(
        [both[:, :128].reshape(n, 8, 128), both[:, 128:].reshape(n, 8, 128)], axis=1
    ).astype(bf16)
    s1[...] = both
    r1[me] = s1[me]
    pl.semaphore_wait(barrier, n - 1)
    scatter(0, s1, r1, False)

    wg = load("wg")[...]
    gating = sigmoid(mul(normed, wg, nn_dims)).astype(bf16).astype(f32)
    cot = load("cot")[...].reshape(cells, 128)
    wc_ref = load("wc")
    dact_ref[...] = mul(cot, wc_ref[...], nt_dims).astype(bf16)
    lane64 = iota((128, 64), 1)
    row64 = iota((128, 64), 0) // 4
    first = low_half(128)

    def spread(vector):
        low = jnp.sum(jnp.where(lane64 == row64, vector, 0.0), axis=1, keepdims=True)
        high = jnp.sum(jnp.where(lane64 == row64 + 32, vector, 0.0), axis=1, keepdims=True)
        return jnp.where(first, low, high).reshape(n, 8, 128)

    gain_e, shift_e = spread(load("gain_e")[...]), spread(load("shift_e")[...])
    gain2, shift2 = load("gain2")[...], load("shift2")[...]
    wo, wx_ref = load("wo")[...], load("wx")
    by_pair = one_hot(col == ((row % 64) // 4) * 8 + (row // 64) * 4 + row % 4)
    pair_rows = one_hot(row == ((col % 64) // 4) * 8 + (col // 64) * 4 + col % 4)
    even = (iota((128, 128), 0) // 4) % 2 == 0

    arrive(0, r1)
    got = r1[...].astype(f32)
    left_all = got[:, :8].reshape(128, 128)
    right_all = mul(by_pair, got[:, 8:].reshape(128, 128).astype(bf16), nn_dims)
    first64 = low_half(64)

    def diagonal(x):
        return jnp.concatenate([jnp.where(first64, x, 0.0), jnp.where(first64, 0.0, x)], axis=0)

    diag0 = diagonal(right_all[:64]).astype(bf16)
    diag1 = diagonal(right_all[64:]).astype(bf16)

    def by_parity(x):
        return jnp.where(even, x, 0.0).astype(bf16), jnp.where(even, 0.0, x).astype(bf16)

    left0, left1 = by_parity(left_all)
    edges = mul(left0, diag0, nt_dims) + mul(left1, diag1, nt_dims)
    s2[...] = edges.reshape(n, 8, 128)
    r2[me] = s2[me]
    scatter(1, s2, r2, False)
    left_bf = left_all.astype(bf16)
    arrive(1, r2)

    edges_in = r2[...]
    inv_c = 1.0 / 64
    centred_e = edges_in - channel_sum(edges_in) * inv_c
    rstd_e = lax.rsqrt(channel_sum(centred_e * centred_e) * inv_c + epsilon)
    hat_e = centred_e * rstd_e
    edge_normed = (hat_e * gain_e + shift_e).reshape(128, 128).astype(bf16)
    edge_normed = unpack(mul(from_owner, edge_normed, nn_dims)).astype(bf16)
    update = mul(edge_normed, wo, tn_dims)
    middle = (state + gating * update).astype(bf16).astype(f32)
    centred2 = middle - jnp.mean(middle, axis=1, keepdims=True)
    rstd2 = lax.rsqrt(jnp.mean(centred2 * centred2, axis=1, keepdims=True) + epsilon)
    hat2 = centred2 * rstd2
    normed2 = (hat2 * gain2 + shift2).astype(bf16)
    units = wc_ref.shape[0]
    dnormed2 = jnp.zeros((cells, 128), f32)
    for begin in range(0, units, 256):
        w_swish = wx_ref[:, begin : begin + 256]
        w_linear = wx_ref[:, units + begin : units + begin + 256]
        swish_in = mul(normed2, w_swish, nn_dims)
        linear = mul(normed2, w_linear, nn_dims)
        dact = dact_ref[:, begin : begin + 256].astype(f32)
        sig = sigmoid(swish_in)
        silu = swish_in * sig
        dlinear = (dact * silu).astype(bf16)
        dswish = (dact * linear * (sig + silu * (1.0 - sig))).astype(bf16)
        dnormed2 = dnormed2 + mul(dswish, w_swish, nt_dims) + mul(dlinear, w_linear, nt_dims)
    dnormed2 = dnormed2.astype(bf16).astype(f32)
    dhat2 = dnormed2 * gain2
    dmiddle = rstd2 * (
        dhat2
        - jnp.mean(dhat2, axis=1, keepdims=True)
        - hat2 * jnp.mean(dhat2 * hat2, axis=1, keepdims=True)
    )
    late = (cot.astype(f32) + dmiddle).astype(bf16).astype(f32)
    dedge = mul(wo, (late * gating).astype(bf16), nt_dims)
    dedge = pack(dedge).astype(bf16)
    dedge = mul(to_owner, dedge, nn_dims).reshape(n, 8, 128)
    dhat_e = dedge * gain_e
    edge_raw = rstd_e * (
        dhat_e - channel_sum(dhat_e) * inv_c - hat_e * (channel_sum(dhat_e * hat_e) * inv_c)
    )
    s3[...] = edge_raw.astype(bf16).astype(f32)
    r3[me] = s3[me]
    scatter(2, s3, r3, False)

    gate_grad = (late * update).astype(bf16).astype(f32)
    dgate = (gate_grad * gating * (1.0 - gating)).astype(bf16)
    dnormed = mul(dgate, wg, nt_dims)
    gain2_sum = jnp.sum(dnormed2 * hat2, axis=0, keepdims=True)
    shift2_sum = jnp.sum(dnormed2, axis=0, keepdims=True)

    def collect(x):
        x = x.reshape(128, 128)
        low = jnp.sum(jnp.where(first, x, 0.0), axis=1, keepdims=True)
        high = jnp.sum(jnp.where(first, 0.0, x), axis=1, keepdims=True)
        spot = row // 4
        return jnp.sum(
            jnp.where(col == spot, low, 0.0) + jnp.where(col == spot + 32, high, 0.0),
            axis=0,
            keepdims=True,
        )

    gain_e_sum = collect(dedge * hat_e)
    shift_e_sum = collect(dedge)
    dsig_l = val_l * sig_l * (1.0 - sig_l) * valid
    dsig_r = val_r * sig_r * (1.0 - sig_r) * valid
    dval_l, dval_r = sig_l * valid, sig_r * valid

    arrive(2, r3)
    edge_round = r3[...].reshape(128, 128)
    round0, round1 = by_parity(edge_round)
    left_grad = mul(round0, diag0, nn_dims) + mul(round1, diag1, nn_dims)
    cross0 = mul(round0, left_bf, tn_dims)
    cross1 = mul(round1, left_bf, tn_dims)
    right_grad = jnp.concatenate(
        [
            jnp.where(first64, cross0[:64], cross0[64:]),
            jnp.where(first64, cross1[:64], cross1[64:]),
        ],
        axis=0,
    ).astype(bf16)
    right_grad = mul(pair_rows, right_grad, nn_dims)
    s4[...] = jnp.concatenate(
        [left_grad.reshape(n, 8, 128), right_grad.reshape(n, 8, 128)], axis=1
    ).astype(bf16)
    r4[me] = s4[me]
    scatter(3, s4, r4, False)
    arrive(3, r4)

    grads = r4[...].astype(f32)
    grads = jnp.concatenate(
        [grads[:, :8].reshape(128, 128), grads[:, 8:].reshape(128, 128)], axis=1
    ).astype(bf16)
    grads = mul(from_owner, grads, nn_dims)
    dleft, dright = unpack(grads[:, :128]), unpack(grads[:, 128:])
    dmixed = jnp.concatenate(
        [dleft * dsig_l, dleft * dval_l, dright * dsig_r, dright * dval_r], axis=0
    ).astype(bf16)
    dnormed = (dnormed + mul(dmixed, we_t, tn_dims)).astype(bf16).astype(f32)
    gain1_sum = jnp.sum(dnormed * hat1, axis=0, keepdims=True)
    shift1_sum = jnp.sum(dnormed, axis=0, keepdims=True)
    blank = jnp.zeros((2, 128), f32)
    s5[...] = jnp.concatenate(
        [gain1_sum, shift1_sum, gain2_sum, shift2_sum, gain_e_sum, shift_e_sum, blank], axis=0
    )
    r5[me] = s5[...]
    scatter(4, s5, r5, True)
    dhat1 = dnormed * gain1
    early = rstd1 * (
        dhat1
        - jnp.mean(dhat1, axis=1, keepdims=True)
        - hat1 * jnp.mean(dhat1 * hat1, axis=1, keepdims=True)
    )
    early = early.astype(bf16).astype(f32)
    out_ref[...] = (early + late).astype(bf16).reshape(out_ref.shape)
    arrive(4, r5)
    sums = jnp.sum(r5[...], axis=0) * (1.0 / tokens)
    norm_ref[...] = sums[:4]
    edge_ref[...] = sums[4:6, :64]
    for phase, buffer in enumerate((r1, r2, r3, r4, r5)):
        sent(phase, buffer)


def fused_body(n, *args):
    (
        pair_state,
        cotangent,
        pair_mask,
        token_count,
        norm_gain,
        norm_shift,
        w_edges,
        w_gate,
        edge_gain,
        edge_shift,
        w_out,
        final_gain,
        final_shift,
        w_expand,
        w_contract,
    ) = args
    vmem = pl.BlockSpec(memory_space=pltpu.VMEM)
    operands = (
        pair_state,
        w_edges,
        norm_gain.reshape(1, -1),
        norm_shift.reshape(1, -1),
        pair_mask,
        token_count.reshape(1, 1),
        w_gate,
        cotangent,
        w_contract,
        edge_gain.reshape(1, -1),
        edge_shift.reshape(1, -1),
        w_out,
        final_gain.reshape(1, -1),
        final_shift.reshape(1, -1),
        w_expand,
    )
    cells = pair_state.shape[0] * pair_state.shape[1]
    tile = pltpu.VMEM((n, 8, 128), f32)
    pair = pltpu.VMEM((n, 16, 128), bf16)
    return pl.pallas_call(
        functools.partial(fused_kernel, n),
        out_shape=(
            jax.ShapeDtypeStruct(pair_state.shape, bf16),
            jax.ShapeDtypeStruct((4, 128), f32),
            jax.ShapeDtypeStruct((2, 64), f32),
        ),
        in_specs=[pl.BlockSpec(memory_space=pltpu.HBM)] * len(operands),
        out_specs=(vmem, vmem, vmem),
        scratch_shapes=[pltpu.VMEM(x.shape, x.dtype) for x in operands]
        + [
            pair,
            pair,
            tile,
            tile,
            tile,
            tile,
            pair,
            pair,
            pltpu.VMEM((8, 128), f32),
            tile,
            pltpu.VMEM((cells, w_contract.shape[0]), bf16),
            pltpu.SemaphoreType.DMA((5,)),
            pltpu.SemaphoreType.DMA((5,)),
            pltpu.SemaphoreType.DMA((len(operands),)),
        ],
        compiler_params=pltpu.CompilerParams(
            collective_id=0, has_side_effects=True, vmem_limit_bytes=60 * 1024 * 1024
        ),
    )(*operands)


def pick_body(n):
    def chosen(*args):
        rows, tokens, _ = args[0].shape
        if (n, rows, tokens) == (16, 4, 64):
            return fused_body(n, *args)
        return body(*args)

    return chosen


def solution(mesh):
    in_specs = (
        P(("groups", "dap"), None, None),
        P(("groups", "dap"), None, None),
        P(("groups", "dap"), None),
        P("groups"),
        P(),
        P(),
        P(),
        P(),
        P(),
        P(),
        P(),
        P(),
        P(),
        P(),
        P(),
    )
    out_specs = (P(("groups", "dap"), None, None), P("groups", None), P("groups", None))
    chosen = pick_body(mesh.shape["dap"])
    return jax.shard_map(chosen, mesh=mesh, in_specs=in_specs, out_specs=out_specs, check_vma=False)
```

```python
import functools

import jax
import jax.numpy as jnp
from jax import lax
from jax.experimental import pallas as pl
from jax.experimental.pallas import tpu as pltpu
from jax.sharding import PartitionSpec as P

epsilon = 1e-05
block_cols = 64


def layer_norm(values, norm_scale, norm_offset):
    centre = jnp.mean(values, axis=-1, keepdims=True)
    centred = values - centre
    spread = jnp.mean(centred * centred, axis=-1, keepdims=True)
    return centred * lax.rsqrt(spread + epsilon) * norm_scale + norm_offset


def project_edges(state, validity, scale_in, offset_in, w_edges, w_gate):
    normed = layer_norm(state.astype(jnp.float32), scale_in, offset_in).astype(jnp.bfloat16)
    channels = w_edges.shape[1] // 4
    mixed = jnp.dot(normed, w_edges, preferred_element_type=jnp.float32)
    weight_mask = validity[..., None]
    left_edges = (
        jax.nn.sigmoid(mixed[..., :channels]) * mixed[..., channels : 2 * channels] * weight_mask
    )
    right_edges = (
        jax.nn.sigmoid(mixed[..., 2 * channels : 3 * channels])
        * mixed[..., 3 * channels :]
        * weight_mask
    )
    gating = jax.nn.sigmoid(jnp.dot(normed, w_gate, preferred_element_type=jnp.float32))
    return (
        left_edges.astype(jnp.bfloat16),
        right_edges.astype(jnp.bfloat16),
        gating.astype(jnp.bfloat16),
    )


def finish_block(
    state,
    edges,
    gating,
    edge_scale,
    edge_offset,
    final_scale,
    final_offset,
    w_out,
    w_expand,
    w_contract,
):
    edge_normed = layer_norm(edges, edge_scale, edge_offset).astype(jnp.bfloat16)
    update = gating.astype(jnp.float32) * jnp.dot(
        edge_normed, w_out, preferred_element_type=jnp.float32
    )
    middle = (state.astype(jnp.float32) + update).astype(jnp.bfloat16).astype(jnp.float32)
    normed = layer_norm(middle, final_scale, final_offset).astype(jnp.bfloat16)
    expanded = jnp.dot(normed, w_expand, preferred_element_type=jnp.float32)
    hidden_units = w_contract.shape[0]
    activated = (jax.nn.silu(expanded[..., :hidden_units]) * expanded[..., hidden_units:]).astype(
        jnp.bfloat16
    )
    return middle + jnp.dot(activated, w_contract, preferred_element_type=jnp.float32)


def body(
    pair_state,
    cotangent,
    pair_mask,
    token_count,
    norm_gain,
    norm_shift,
    w_edges,
    w_gate,
    edge_gain,
    edge_shift,
    w_out,
    final_gain,
    final_shift,
    w_expand,
    w_contract,
):
    rows_dev = pair_state.shape[0]
    tokens_all = pair_state.shape[1]
    first_row = lax.axis_index("dap") * rows_dev
    row_ids = first_row + jnp.arange(rows_dev, dtype=jnp.int32)
    column_ids = jnp.arange(tokens_all, dtype=jnp.int32)
    live_count = token_count[0]
    validity = (
        pair_mask.astype(jnp.float32)
        * (row_ids < live_count).astype(jnp.float32)[:, None]
        * (column_ids < live_count).astype(jnp.float32)[None, :]
    )

    def project_local(state_in, scale_in, offset_in):
        return project_edges(state_in, validity, scale_in, offset_in, w_edges, w_gate)

    outputs, project_back = jax.vjp(project_local, pair_state, norm_gain, norm_shift)
    left_edges, right_edges, gating = lax.optimization_barrier(outputs)
    left_rows = left_edges.transpose(2, 0, 1)
    right_rows = right_edges.transpose(2, 0, 1)
    channels = left_rows.shape[0]

    def finish_local(state_in, edges_in, gate_in, scale_a, offset_a, scale_b, offset_b):
        return finish_block(
            state_in,
            edges_in,
            gate_in,
            scale_a,
            offset_a,
            scale_b,
            offset_b,
            w_out,
            w_expand,
            w_contract,
        )

    def absorb_block(carry_in, piece_rows, offset_at):
        left_grad, edge_grads_all, state_grad, gate_grad, norm_sums = carry_in
        width_now = piece_rows.shape[1]
        edges = jnp.einsum(
            "cik,cjk->cij", left_rows, piece_rows, preferred_element_type=jnp.float32
        )
        state_part = lax.dynamic_slice_in_dim(pair_state, offset_at, width_now, 1)
        gate_part = lax.dynamic_slice_in_dim(gating, offset_at, width_now, 1)
        cotan_part = lax.dynamic_slice_in_dim(cotangent, offset_at, width_now, 1)
        _, finish_back = jax.vjp(
            finish_local,
            state_part,
            edges.transpose(1, 2, 0),
            gate_part,
            edge_gain,
            edge_shift,
            final_gain,
            final_shift,
        )
        grads = finish_back(cotan_part.astype(jnp.float32))
        edge_round = grads[1].transpose(2, 0, 1).astype(jnp.bfloat16)
        left_grad = left_grad + jnp.einsum(
            "cij,cjk->cik", edge_round, piece_rows, preferred_element_type=jnp.float32
        )
        edge_grads_all = lax.dynamic_update_slice_in_dim(edge_grads_all, edge_round, offset_at, 2)
        state_grad = lax.dynamic_update_slice_in_dim(state_grad, grads[0], offset_at, 1)
        gate_grad = lax.dynamic_update_slice_in_dim(gate_grad, grads[2], offset_at, 1)
        norm_sums = (
            norm_sums[0] + grads[3],
            norm_sums[1] + grads[4],
            norm_sums[2] + grads[5],
            norm_sums[3] + grads[6],
        )
        return (left_grad, edge_grads_all, state_grad, gate_grad, norm_sums)

    def absorb(carry_in, piece_rows, offset_at):
        width_now = piece_rows.shape[1]
        if width_now > block_cols and width_now % block_cols == 0:

            def step_block(index_at, carry_now):
                begin = index_at * block_cols
                part_rows = lax.dynamic_slice_in_dim(piece_rows, begin, block_cols, 1)
                return absorb_block(carry_now, part_rows, offset_at + begin)

            return lax.fori_loop(0, width_now // block_cols, step_block, carry_in)
        return absorb_block(carry_in, piece_rows, offset_at)

    start_carry = (
        jnp.zeros((channels, rows_dev, tokens_all), jnp.float32),
        jnp.zeros((channels, rows_dev, tokens_all), jnp.bfloat16),
        jnp.zeros(pair_state.shape, jnp.bfloat16),
        jnp.zeros(gating.shape, jnp.bfloat16),
        (
            jnp.zeros(edge_gain.shape, jnp.float32),
            jnp.zeros(edge_shift.shape, jnp.float32),
            jnp.zeros(final_gain.shape, jnp.float32),
            jnp.zeros(final_shift.shape, jnp.float32),
        ),
    )
    left_sum, edge_grads_all, late_grad, gate_grad, norm_sums = absorb(
        start_carry, lax.all_gather(right_rows, "dap", axis=1, tiled=True), jnp.int32(0)
    )
    left_grad = left_sum.astype(jnp.bfloat16)
    columns = lax.all_to_all(edge_grads_all, "dap", split_axis=2, concat_axis=1, tiled=True)
    piece_rows = lax.all_gather(left_rows, "dap", axis=1, tiled=True)
    width_now = piece_rows.shape[1]
    right_sum = jnp.einsum("cij,cik->cjk", columns, piece_rows, preferred_element_type=jnp.float32)
    right_grad = right_sum.astype(jnp.bfloat16)
    cotangents = lax.optimization_barrier(
        (left_grad.transpose(1, 2, 0), right_grad.transpose(1, 2, 0), gate_grad)
    )
    early_grad, gain_grad, shift_grad = project_back(cotangents)
    summed = lax.optimization_barrier((early_grad, late_grad))
    grad_pair = (summed[0].astype(jnp.float32) + summed[1].astype(jnp.float32)).astype(jnp.bfloat16)
    pair_terms = jnp.stack([gain_grad, shift_grad, norm_sums[2], norm_sums[3]])
    edge_terms = jnp.stack([norm_sums[0], norm_sums[1]])
    pair_totals, edge_totals = lax.psum((pair_terms, edge_terms), "dap")
    return (grad_pair, pair_totals / tokens_all, edge_totals / tokens_all)

nn_dims = (((1,), (0,)), ((), ()))
nt_dims = (((1,), (1,)), ((), ()))
tn_dims = (((0,), (0,)), ((), ()))
f32 = jnp.float32
bf16 = jnp.bfloat16


def mul(a, b, dims):
    return lax.dot_general(a, b, dims, preferred_element_type=f32)


def sigmoid(x):
    return 0.5 * jnp.tanh(0.5 * x) + 0.5


def iota(shape, axis):
    return lax.broadcasted_iota(jnp.int32, shape, axis)


def low_half(rows):
    return iota((rows, 128), 1) < 64


def pack(x):
    low, high = x[:32], x[32:]
    first = low_half(32)
    pieces = []
    for half in range(2):
        a, b = low[:, half * 128 : half * 128 + 128], high[:, half * 128 : half * 128 + 128]
        pieces.append(jnp.where(first, a, pltpu.roll(b, 64, 1)))
        pieces.append(jnp.where(first, pltpu.roll(a, 64, 1), b))
    return jnp.concatenate(pieces, axis=0)


def unpack(x):
    first = low_half(32)
    lows, highs = [], []
    for half in range(2):
        a, b = x[half * 64 : half * 64 + 32], x[half * 64 + 32 : half * 64 + 64]
        lows.append(jnp.where(first, a, pltpu.roll(b, 64, 1)))
        highs.append(jnp.where(first, pltpu.roll(a, 64, 1), b))
    return jnp.concatenate(
        [jnp.concatenate(lows, axis=1), jnp.concatenate(highs, axis=1)], axis=0
    )


def one_hot(hit):
    return jnp.where(hit, 1.0, 0.0).astype(bf16)


def channel_sum(x):
    total = jnp.sum(x, axis=0)
    total = total + pltpu.roll(total, 4, 0)
    return total + pltpu.roll(total, 64, 1)


names = (
    "state",
    "we",
    "gain1",
    "shift1",
    "mask",
    "real",
    "wg",
    "cot",
    "wc",
    "gain_e",
    "shift_e",
    "wo",
    "gain2",
    "shift2",
    "wx",
)


def fused_kernel(n, *refs):
    count = len(names)
    sources, refs = refs[:count], refs[count:]
    out_ref, norm_ref, edge_ref, *held = refs[: 3 + count]
    s1, r1, s2, r2, s3, r3, s4, r4, s5, r5, dact_ref, send_sem, recv_sem, load_sem = refs[3 + count :]
    me = lax.axis_index("dap")
    group = lax.axis_index("groups")
    loads = {
        name: pltpu.make_async_copy(sources[at], held[at], load_sem.at[at])
        for at, name in enumerate(names)
    }
    for name in names:
        loads[name].start()

    def load(name):
        loads[name].wait()
        return held[names.index(name)]

    rows, tokens = sources[0].shape[:2]
    cells = rows * tokens

    barrier = pltpu.get_barrier_semaphore()

    high, y, core = me // 8, (me // 2) % 2, me % 2
    z = me // 4
    peers = []
    for far in (3 - 3 * high, 2 - high, 1 - z + 4 * high):
        for side in (1 - y, y):
            peers += [far * 4 + side * 2 + 1 - core, far * 4 + side * 2 + core]
    peers += [z * 4 + (1 - y) * 2 + 1 - core, z * 4 + (1 - y) * 2 + core, z * 4 + y * 2 + 1 - core]

    for peer in peers:
        pl.semaphore_signal(
            barrier, inc=1, device_id=(group, peer), device_id_type=pl.DeviceIdType.MESH
        )

    def scatter(phase, src, dst, same):
        for peer in peers:
            pltpu.make_async_remote_copy(
                src_ref=src if same else src.at[peer],
                dst_ref=dst.at[me],
                send_sem=send_sem.at[phase],
                recv_sem=recv_sem.at[phase],
                device_id=(group, peer),
                device_id_type=pl.DeviceIdType.MESH,
            ).start()

    def arrive(phase, dst):
        part = dst.at[pl.ds(0, n - 1)]
        pltpu.make_async_copy(part, part, recv_sem.at[phase]).wait()

    def sent(phase, dst):
        part = dst.at[pl.ds(0, n - 1)]
        pltpu.make_async_copy(part, part, send_sem.at[phase]).wait()

    state = load("state")[...].reshape(cells, 128).astype(f32)
    gain1 = load("gain1")[...]
    centred = state - jnp.mean(state, axis=1, keepdims=True)
    rstd1 = lax.rsqrt(jnp.mean(centred * centred, axis=1, keepdims=True) + epsilon)
    hat1 = centred * rstd1
    normed = (hat1 * gain1 + load("shift1")[...]).astype(bf16)
    we_t = load("we")[...].T
    mixed = mul(we_t, normed, nt_dims)
    real = load("real")[...]
    mask = load("mask")[...].astype(f32)
    mask = jnp.concatenate([mask[i : i + 1] for i in range(rows)], axis=1)
    cell = iota((1, cells), 1)
    live = (cell % tokens < real) & (me * rows + cell // tokens < real)
    valid = jnp.where(live, mask, 0.0)
    sig_l, val_l = sigmoid(mixed[:64]), mixed[64:128]
    sig_r, val_r = sigmoid(mixed[128:192]), mixed[192:]
    left = pack(sig_l * val_l * valid).astype(bf16)
    right = pack(sig_r * val_r * valid).astype(bf16)
    row, col = iota((128, 128), 0), iota((128, 128), 1)
    to_owner = one_hot(col == (row % 4) * 32 + (row // 8) * 2 + (row // 4) % 2)
    from_owner = one_hot(row == (col % 4) * 32 + (col // 8) * 2 + (col // 4) % 2)
    both = mul(to_owner, jnp.concatenate([left, right], axis=1), nn_dims)
    both = jnp.concatenate(
        [both[:, :128].reshape(n, 8, 128), both[:, 128:].reshape(n, 8, 128)], axis=1
    ).astype(bf16)
    s1[...] = both
    r1[me] = s1[me]
    pl.semaphore_wait(barrier, n - 1)
    scatter(0, s1, r1, False)

    wg = load("wg")[...]
    gating = sigmoid(mul(normed, wg, nn_dims)).astype(bf16).astype(f32)
    cot = load("cot")[...].reshape(cells, 128)
    wc_ref = load("wc")
    dact_ref[...] = mul(cot, wc_ref[...], nt_dims).astype(bf16)
    lane64 = iota((128, 64), 1)
    row64 = iota((128, 64), 0) // 4
    first = low_half(128)

    def spread(vector):
        low = jnp.sum(jnp.where(lane64 == row64, vector, 0.0), axis=1, keepdims=True)
        high = jnp.sum(jnp.where(lane64 == row64 + 32, vector, 0.0), axis=1, keepdims=True)
        return jnp.where(first, low, high).reshape(n, 8, 128)

    gain_e, shift_e = spread(load("gain_e")[...]), spread(load("shift_e")[...])
    gain2, shift2 = load("gain2")[...], load("shift2")[...]
    wo, wx_ref = load("wo")[...], load("wx")
    by_pair = one_hot(col == ((row % 64) // 4) * 8 + (row // 64) * 4 + row % 4)
    pair_rows = one_hot(row == ((col % 64) // 4) * 8 + (col // 64) * 4 + col % 4)
    even = (iota((128, 128), 0) // 4) % 2 == 0

    arrive(0, r1)
    got = r1[...].astype(f32)
    left_all = got[:, :8].reshape(128, 128)
    right_all = mul(by_pair, got[:, 8:].reshape(128, 128).astype(bf16), nn_dims)
    first64 = low_half(64)

    def diagonal(x):
        return jnp.concatenate([jnp.where(first64, x, 0.0), jnp.where(first64, 0.0, x)], axis=0)

    diag0 = diagonal(right_all[:64]).astype(bf16)
    diag1 = diagonal(right_all[64:]).astype(bf16)

    def by_parity(x):
        return jnp.where(even, x, 0.0).astype(bf16), jnp.where(even, 0.0, x).astype(bf16)

    left0, left1 = by_parity(left_all)
    edges = mul(left0, diag0, nt_dims) + mul(left1, diag1, nt_dims)
    s2[...] = edges.reshape(n, 8, 128)
    r2[me] = s2[me]
    scatter(1, s2, r2, False)
    left_bf = left_all.astype(bf16)
    arrive(1, r2)

    edges_in = r2[...]
    inv_c = 1.0 / 64
    centred_e = edges_in - channel_sum(edges_in) * inv_c
    rstd_e = lax.rsqrt(channel_sum(centred_e * centred_e) * inv_c + epsilon)
    hat_e = centred_e * rstd_e
    edge_normed = (hat_e * gain_e + shift_e).reshape(128, 128).astype(bf16)
    edge_normed = unpack(mul(from_owner, edge_normed, nn_dims)).astype(bf16)
    update = mul(edge_normed, wo, tn_dims)
    middle = (state + gating * update).astype(bf16).astype(f32)
    centred2 = middle - jnp.mean(middle, axis=1, keepdims=True)
    rstd2 = lax.rsqrt(jnp.mean(centred2 * centred2, axis=1, keepdims=True) + epsilon)
    hat2 = centred2 * rstd2
    normed2 = (hat2 * gain2 + shift2).astype(bf16)
    units = wc_ref.shape[0]
    dnormed2 = jnp.zeros((cells, 128), f32)
    for begin in range(0, units, 256):
        w_swish = wx_ref[:, begin : begin + 256]
        w_linear = wx_ref[:, units + begin : units + begin + 256]
        swish_in = mul(normed2, w_swish, nn_dims)
        linear = mul(normed2, w_linear, nn_dims)
        dact = dact_ref[:, begin : begin + 256].astype(f32)
        sig = sigmoid(swish_in)
        silu = swish_in * sig
        dlinear = (dact * silu).astype(bf16)
        dswish = (dact * linear * (sig + silu * (1.0 - sig))).astype(bf16)
        dnormed2 = dnormed2 + mul(dswish, w_swish, nt_dims) + mul(dlinear, w_linear, nt_dims)
    dnormed2 = dnormed2.astype(bf16).astype(f32)
    dhat2 = dnormed2 * gain2
    dmiddle = rstd2 * (
        dhat2
        - jnp.mean(dhat2, axis=1, keepdims=True)
        - hat2 * jnp.mean(dhat2 * hat2, axis=1, keepdims=True)
    )
    late = (cot.astype(f32) + dmiddle).astype(bf16).astype(f32)
    dedge = mul(wo, (late * gating).astype(bf16), nt_dims)
    dedge = pack(dedge).astype(bf16)
    dedge = mul(to_owner, dedge, nn_dims).reshape(n, 8, 128)
    dhat_e = dedge * gain_e
    edge_raw = rstd_e * (
        dhat_e - channel_sum(dhat_e) * inv_c - hat_e * (channel_sum(dhat_e * hat_e) * inv_c)
    )
    s3[...] = edge_raw.astype(bf16).astype(f32)
    r3[me] = s3[me]
    scatter(2, s3, r3, False)

    gate_grad = (late * update).astype(bf16).astype(f32)
    dgate = (gate_grad * gating * (1.0 - gating)).astype(bf16)
    dnormed = mul(dgate, wg, nt_dims)
    gain2_sum = jnp.sum(dnormed2 * hat2, axis=0, keepdims=True)
    shift2_sum = jnp.sum(dnormed2, axis=0, keepdims=True)

    def collect(x):
        x = x.reshape(128, 128)
        low = jnp.sum(jnp.where(first, x, 0.0), axis=1, keepdims=True)
        high = jnp.sum(jnp.where(first, 0.0, x), axis=1, keepdims=True)
        spot = row // 4
        return jnp.sum(
            jnp.where(col == spot, low, 0.0) + jnp.where(col == spot + 32, high, 0.0),
            axis=0,
            keepdims=True,
        )

    gain_e_sum = collect(dedge * hat_e)
    shift_e_sum = collect(dedge)
    dsig_l = val_l * sig_l * (1.0 - sig_l) * valid
    dsig_r = val_r * sig_r * (1.0 - sig_r) * valid
    dval_l, dval_r = sig_l * valid, sig_r * valid

    arrive(2, r3)
    edge_round = r3[...].reshape(128, 128)
    round0, round1 = by_parity(edge_round)
    left_grad = mul(round0, diag0, nn_dims) + mul(round1, diag1, nn_dims)
    cross0 = mul(round0, left_bf, tn_dims)
    cross1 = mul(round1, left_bf, tn_dims)
    right_grad = jnp.concatenate(
        [
            jnp.where(first64, cross0[:64], cross0[64:]),
            jnp.where(first64, cross1[:64], cross1[64:]),
        ],
        axis=0,
    ).astype(bf16)
    right_grad = mul(pair_rows, right_grad, nn_dims)
    s4[...] = jnp.concatenate(
        [left_grad.reshape(n, 8, 128), right_grad.reshape(n, 8, 128)], axis=1
    ).astype(bf16)
    r4[me] = s4[me]
    scatter(3, s4, r4, False)
    arrive(3, r4)

    grads = r4[...].astype(f32)
    grads = jnp.concatenate(
        [grads[:, :8].reshape(128, 128), grads[:, 8:].reshape(128, 128)], axis=1
    ).astype(bf16)
    grads = mul(from_owner, grads, nn_dims)
    dleft, dright = unpack(grads[:, :128]), unpack(grads[:, 128:])
    dmixed = jnp.concatenate(
        [dleft * dsig_l, dleft * dval_l, dright * dsig_r, dright * dval_r], axis=0
    ).astype(bf16)
    dnormed = (dnormed + mul(dmixed, we_t, tn_dims)).astype(bf16).astype(f32)
    gain1_sum = jnp.sum(dnormed * hat1, axis=0, keepdims=True)
    shift1_sum = jnp.sum(dnormed, axis=0, keepdims=True)
    blank = jnp.zeros((2, 128), f32)
    s5[...] = jnp.concatenate(
        [gain1_sum, shift1_sum, gain2_sum, shift2_sum, gain_e_sum, shift_e_sum, blank], axis=0
    )
    r5[me] = s5[...]
    scatter(4, s5, r5, True)
    dhat1 = dnormed * gain1
    early = rstd1 * (
        dhat1
        - jnp.mean(dhat1, axis=1, keepdims=True)
        - hat1 * jnp.mean(dhat1 * hat1, axis=1, keepdims=True)
    )
    early = early.astype(bf16).astype(f32)
    out_ref[...] = (early + late).astype(bf16).reshape(out_ref.shape)
    arrive(4, r5)
    sums = jnp.sum(r5[...], axis=0) * (1.0 / tokens)
    norm_ref[...] = sums[:4]
    edge_ref[...] = sums[4:6, :64]
    for phase, buffer in enumerate((r1, r2, r3, r4, r5)):
        sent(phase, buffer)


def write_out(a, b, c, out_a, out_b, out_c, sem):
    copies = [
        pltpu.make_async_copy(source, target, sem.at[at])
        for at, (source, target) in enumerate(((a, out_a), (b, out_b), (c, out_c)))
    ]
    for copy in copies:
        copy.start()
    for copy in copies:
        copy.wait()


def fused_body(n, *args):
    (
        pair_state,
        cotangent,
        pair_mask,
        token_count,
        norm_gain,
        norm_shift,
        w_edges,
        w_gate,
        edge_gain,
        edge_shift,
        w_out,
        final_gain,
        final_shift,
        w_expand,
        w_contract,
    ) = args
    vmem = pl.BlockSpec(memory_space=pltpu.VMEM)
    operands = (
        pair_state,
        w_edges,
        norm_gain.reshape(1, -1),
        norm_shift.reshape(1, -1),
        pair_mask,
        token_count.reshape(1, 1),
        w_gate,
        cotangent,
        w_contract,
        edge_gain.reshape(1, -1),
        edge_shift.reshape(1, -1),
        w_out,
        final_gain.reshape(1, -1),
        final_shift.reshape(1, -1),
        w_expand,
    )
    cells = pair_state.shape[0] * pair_state.shape[1]
    tile = pltpu.VMEM((n, 8, 128), f32)
    pair = pltpu.VMEM((n, 16, 128), bf16)
    held = pl.pallas_call(
        functools.partial(fused_kernel, n),
        out_shape=(
            pltpu.VMEM(pair_state.shape, bf16),
            pltpu.VMEM((4, 128), f32),
            pltpu.VMEM((2, 64), f32),
        ),
        in_specs=[pl.BlockSpec(memory_space=pltpu.HBM)] * len(operands),
        out_specs=(vmem, vmem, vmem),
        scratch_shapes=[pltpu.VMEM(x.shape, x.dtype) for x in operands]
        + [
            pair,
            pair,
            tile,
            tile,
            tile,
            tile,
            pair,
            pair,
            pltpu.VMEM((8, 128), f32),
            tile,
            pltpu.VMEM((cells, w_contract.shape[0]), bf16),
            pltpu.SemaphoreType.DMA((5,)),
            pltpu.SemaphoreType.DMA((5,)),
            pltpu.SemaphoreType.DMA((len(operands),)),
        ],
        compiler_params=pltpu.CompilerParams(
            collective_id=0, has_side_effects=True, vmem_limit_bytes=60 * 1024 * 1024
        ),
    )(*operands)
    return pl.pallas_call(
        write_out,
        out_shape=tuple(jax.ShapeDtypeStruct(x.shape, x.dtype) for x in held),
        in_specs=[vmem] * 3,
        out_specs=(pl.BlockSpec(memory_space=pltpu.HBM),) * 3,
        scratch_shapes=[pltpu.SemaphoreType.DMA((3,))],
        compiler_params=pltpu.CompilerParams(vmem_limit_bytes=1024 * 1024),
    )(*held)


def pick_body(n):
    def chosen(*args):
        rows, tokens, _ = args[0].shape
        if (n, rows, tokens) == (16, 4, 64):
            return fused_body(n, *args)
        return body(*args)

    return chosen


def solution(mesh):
    in_specs = (
        P(("groups", "dap"), None, None),
        P(("groups", "dap"), None, None),
        P(("groups", "dap"), None),
        P("groups"),
        P(),
        P(),
        P(),
        P(),
        P(),
        P(),
        P(),
        P(),
        P(),
        P(),
        P(),
    )
    out_specs = (P(("groups", "dap"), None, None), P("groups", None), P("groups", None))
    chosen = pick_body(mesh.shape["dap"])
    return jax.shard_map(chosen, mesh=mesh, in_specs=in_specs, out_specs=out_specs, check_vma=False)
```

```python
import functools

import jax
import jax.numpy as jnp
from jax import lax
from jax.experimental import pallas as pl
from jax.experimental.pallas import tpu as pltpu
from jax.sharding import PartitionSpec as P

epsilon = 1e-05
block_cols = 64


def layer_norm(values, norm_scale, norm_offset):
    centre = jnp.mean(values, axis=-1, keepdims=True)
    centred = values - centre
    spread = jnp.mean(centred * centred, axis=-1, keepdims=True)
    return centred * lax.rsqrt(spread + epsilon) * norm_scale + norm_offset


def project_edges(state, validity, scale_in, offset_in, w_edges, w_gate):
    normed = layer_norm(state.astype(jnp.float32), scale_in, offset_in).astype(jnp.bfloat16)
    channels = w_edges.shape[1] // 4
    mixed = jnp.dot(normed, w_edges, preferred_element_type=jnp.float32)
    weight_mask = validity[..., None]
    left_edges = (
        jax.nn.sigmoid(mixed[..., :channels]) * mixed[..., channels : 2 * channels] * weight_mask
    )
    right_edges = (
        jax.nn.sigmoid(mixed[..., 2 * channels : 3 * channels])
        * mixed[..., 3 * channels :]
        * weight_mask
    )
    gating = jax.nn.sigmoid(jnp.dot(normed, w_gate, preferred_element_type=jnp.float32))
    return (
        left_edges.astype(jnp.bfloat16),
        right_edges.astype(jnp.bfloat16),
        gating.astype(jnp.bfloat16),
    )


def finish_block(
    state,
    edges,
    gating,
    edge_scale,
    edge_offset,
    final_scale,
    final_offset,
    w_out,
    w_expand,
    w_contract,
):
    edge_normed = layer_norm(edges, edge_scale, edge_offset).astype(jnp.bfloat16)
    update = gating.astype(jnp.float32) * jnp.dot(
        edge_normed, w_out, preferred_element_type=jnp.float32
    )
    middle = (state.astype(jnp.float32) + update).astype(jnp.bfloat16).astype(jnp.float32)
    normed = layer_norm(middle, final_scale, final_offset).astype(jnp.bfloat16)
    expanded = jnp.dot(normed, w_expand, preferred_element_type=jnp.float32)
    hidden_units = w_contract.shape[0]
    activated = (jax.nn.silu(expanded[..., :hidden_units]) * expanded[..., hidden_units:]).astype(
        jnp.bfloat16
    )
    return middle + jnp.dot(activated, w_contract, preferred_element_type=jnp.float32)


def body(
    pair_state,
    cotangent,
    pair_mask,
    token_count,
    norm_gain,
    norm_shift,
    w_edges,
    w_gate,
    edge_gain,
    edge_shift,
    w_out,
    final_gain,
    final_shift,
    w_expand,
    w_contract,
):
    rows_dev = pair_state.shape[0]
    tokens_all = pair_state.shape[1]
    first_row = lax.axis_index("dap") * rows_dev
    row_ids = first_row + jnp.arange(rows_dev, dtype=jnp.int32)
    column_ids = jnp.arange(tokens_all, dtype=jnp.int32)
    live_count = token_count[0]
    validity = (
        pair_mask.astype(jnp.float32)
        * (row_ids < live_count).astype(jnp.float32)[:, None]
        * (column_ids < live_count).astype(jnp.float32)[None, :]
    )

    def project_local(state_in, scale_in, offset_in):
        return project_edges(state_in, validity, scale_in, offset_in, w_edges, w_gate)

    outputs, project_back = jax.vjp(project_local, pair_state, norm_gain, norm_shift)
    left_edges, right_edges, gating = lax.optimization_barrier(outputs)
    left_rows = left_edges.transpose(2, 0, 1)
    right_rows = right_edges.transpose(2, 0, 1)
    channels = left_rows.shape[0]

    def finish_local(state_in, edges_in, gate_in, scale_a, offset_a, scale_b, offset_b):
        return finish_block(
            state_in,
            edges_in,
            gate_in,
            scale_a,
            offset_a,
            scale_b,
            offset_b,
            w_out,
            w_expand,
            w_contract,
        )

    def absorb_block(carry_in, piece_rows, offset_at):
        left_grad, edge_grads_all, state_grad, gate_grad, norm_sums = carry_in
        width_now = piece_rows.shape[1]
        edges = jnp.einsum(
            "cik,cjk->cij", left_rows, piece_rows, preferred_element_type=jnp.float32
        )
        state_part = lax.dynamic_slice_in_dim(pair_state, offset_at, width_now, 1)
        gate_part = lax.dynamic_slice_in_dim(gating, offset_at, width_now, 1)
        cotan_part = lax.dynamic_slice_in_dim(cotangent, offset_at, width_now, 1)
        _, finish_back = jax.vjp(
            finish_local,
            state_part,
            edges.transpose(1, 2, 0),
            gate_part,
            edge_gain,
            edge_shift,
            final_gain,
            final_shift,
        )
        grads = finish_back(cotan_part.astype(jnp.float32))
        edge_round = grads[1].transpose(2, 0, 1).astype(jnp.bfloat16)
        left_grad = left_grad + jnp.einsum(
            "cij,cjk->cik", edge_round, piece_rows, preferred_element_type=jnp.float32
        )
        edge_grads_all = lax.dynamic_update_slice_in_dim(edge_grads_all, edge_round, offset_at, 2)
        state_grad = lax.dynamic_update_slice_in_dim(state_grad, grads[0], offset_at, 1)
        gate_grad = lax.dynamic_update_slice_in_dim(gate_grad, grads[2], offset_at, 1)
        norm_sums = (
            norm_sums[0] + grads[3],
            norm_sums[1] + grads[4],
            norm_sums[2] + grads[5],
            norm_sums[3] + grads[6],
        )
        return (left_grad, edge_grads_all, state_grad, gate_grad, norm_sums)

    def absorb(carry_in, piece_rows, offset_at):
        width_now = piece_rows.shape[1]
        if width_now > block_cols and width_now % block_cols == 0:

            def step_block(index_at, carry_now):
                begin = index_at * block_cols
                part_rows = lax.dynamic_slice_in_dim(piece_rows, begin, block_cols, 1)
                return absorb_block(carry_now, part_rows, offset_at + begin)

            return lax.fori_loop(0, width_now // block_cols, step_block, carry_in)
        return absorb_block(carry_in, piece_rows, offset_at)

    start_carry = (
        jnp.zeros((channels, rows_dev, tokens_all), jnp.float32),
        jnp.zeros((channels, rows_dev, tokens_all), jnp.bfloat16),
        jnp.zeros(pair_state.shape, jnp.bfloat16),
        jnp.zeros(gating.shape, jnp.bfloat16),
        (
            jnp.zeros(edge_gain.shape, jnp.float32),
            jnp.zeros(edge_shift.shape, jnp.float32),
            jnp.zeros(final_gain.shape, jnp.float32),
            jnp.zeros(final_shift.shape, jnp.float32),
        ),
    )
    left_sum, edge_grads_all, late_grad, gate_grad, norm_sums = absorb(
        start_carry, lax.all_gather(right_rows, "dap", axis=1, tiled=True), jnp.int32(0)
    )
    left_grad = left_sum.astype(jnp.bfloat16)
    columns = lax.all_to_all(edge_grads_all, "dap", split_axis=2, concat_axis=1, tiled=True)
    piece_rows = lax.all_gather(left_rows, "dap", axis=1, tiled=True)
    width_now = piece_rows.shape[1]
    right_sum = jnp.einsum("cij,cik->cjk", columns, piece_rows, preferred_element_type=jnp.float32)
    right_grad = right_sum.astype(jnp.bfloat16)
    cotangents = lax.optimization_barrier(
        (left_grad.transpose(1, 2, 0), right_grad.transpose(1, 2, 0), gate_grad)
    )
    early_grad, gain_grad, shift_grad = project_back(cotangents)
    summed = lax.optimization_barrier((early_grad, late_grad))
    grad_pair = (summed[0].astype(jnp.float32) + summed[1].astype(jnp.float32)).astype(jnp.bfloat16)
    pair_terms = jnp.stack([gain_grad, shift_grad, norm_sums[2], norm_sums[3]])
    edge_terms = jnp.stack([norm_sums[0], norm_sums[1]])
    pair_totals, edge_totals = lax.psum((pair_terms, edge_terms), "dap")
    return (grad_pair, pair_totals / tokens_all, edge_totals / tokens_all)

nn_dims = (((1,), (0,)), ((), ()))
nt_dims = (((1,), (1,)), ((), ()))
tn_dims = (((0,), (0,)), ((), ()))
f32 = jnp.float32
bf16 = jnp.bfloat16


def mul(a, b, dims):
    return lax.dot_general(a, b, dims, preferred_element_type=f32)


def sigmoid(x):
    return 0.5 * jnp.tanh(0.5 * x) + 0.5


def iota(shape, axis):
    return lax.broadcasted_iota(jnp.int32, shape, axis)


def low_half(rows):
    return iota((rows, 128), 1) < 64


def pack(x):
    low, high = x[:32], x[32:]
    first = low_half(32)
    pieces = []
    for half in range(2):
        a, b = low[:, half * 128 : half * 128 + 128], high[:, half * 128 : half * 128 + 128]
        pieces.append(jnp.where(first, a, pltpu.roll(b, 64, 1)))
        pieces.append(jnp.where(first, pltpu.roll(a, 64, 1), b))
    return jnp.concatenate(pieces, axis=0)


def unpack(x):
    first = low_half(32)
    lows, highs = [], []
    for half in range(2):
        a, b = x[half * 64 : half * 64 + 32], x[half * 64 + 32 : half * 64 + 64]
        lows.append(jnp.where(first, a, pltpu.roll(b, 64, 1)))
        highs.append(jnp.where(first, pltpu.roll(a, 64, 1), b))
    return jnp.concatenate(
        [jnp.concatenate(lows, axis=1), jnp.concatenate(highs, axis=1)], axis=0
    )


def one_hot(hit):
    return jnp.where(hit, 1.0, 0.0).astype(bf16)


def channel_sum(x):
    total = jnp.sum(x, axis=0)
    total = total + pltpu.roll(total, 4, 0)
    return total + pltpu.roll(total, 64, 1)


names = (
    "state",
    "we",
    "gain1",
    "shift1",
    "mask",
    "real",
    "wg",
    "cot",
    "wc",
    "gain_e",
    "shift_e",
    "wo",
    "gain2",
    "shift2",
    "wx",
)


def fused_kernel(n, *refs):
    count = len(names)
    sources, refs = refs[:count], refs[count:]
    out_ref, norm_ref, edge_ref, *held = refs[: 3 + count]
    s1, r1, s2, r2, s3, r3, s4, r4, s5, r5, dact_ref, wxt_ref, send_sem, recv_sem, load_sem = refs[3 + count :]
    me = lax.axis_index("dap")
    group = lax.axis_index("groups")
    loads = {
        name: pltpu.make_async_copy(sources[at], held[at], load_sem.at[at])
        for at, name in enumerate(names)
    }
    def load(name):
        loads[name].wait()
        return held[names.index(name)]

    rows, tokens = sources[0].shape[:2]
    cells = rows * tokens

    barrier = pltpu.get_barrier_semaphore()

    high, y, core = me // 8, (me // 2) % 2, me % 2
    z = me // 4
    peers = []
    for far in (3 - 3 * high, 2 - high, 1 - z + 4 * high):
        for side in (1 - y, y):
            peers += [far * 4 + side * 2 + 1 - core, far * 4 + side * 2 + core]
    peers += [z * 4 + (1 - y) * 2 + 1 - core, z * 4 + (1 - y) * 2 + core, z * 4 + y * 2 + 1 - core]

    for peer in peers:
        pl.semaphore_signal(
            barrier, inc=1, device_id=(group, peer), device_id_type=pl.DeviceIdType.MESH
        )

    for name in names:
        loads[name].start()

    def scatter(phase, src, dst, same):
        for peer in peers:
            pltpu.make_async_remote_copy(
                src_ref=src if same else src.at[peer],
                dst_ref=dst.at[me],
                send_sem=send_sem.at[phase],
                recv_sem=recv_sem.at[phase],
                device_id=(group, peer),
                device_id_type=pl.DeviceIdType.MESH,
            ).start()

    def arrive(phase, dst):
        part = dst.at[pl.ds(0, n - 1)]
        pltpu.make_async_copy(part, part, recv_sem.at[phase]).wait()

    def sent(phase, dst):
        part = dst.at[pl.ds(0, n - 1)]
        pltpu.make_async_copy(part, part, send_sem.at[phase]).wait()

    state = load("state")[...].reshape(cells, 128).astype(f32)
    gain1 = load("gain1")[...]
    centred = state - jnp.mean(state, axis=1, keepdims=True)
    rstd1 = lax.rsqrt(jnp.mean(centred * centred, axis=1, keepdims=True) + epsilon)
    hat1 = centred * rstd1
    normed = (hat1 * gain1 + load("shift1")[...]).astype(bf16)
    we_t = load("we")[...].T
    mixed = mul(we_t, normed, nt_dims)
    real = load("real")[...]
    mask = load("mask")[...].astype(f32)
    mask = jnp.concatenate([mask[i : i + 1] for i in range(rows)], axis=1)
    cell = iota((1, cells), 1)
    live = (cell % tokens < real) & (me * rows + cell // tokens < real)
    valid = jnp.where(live, mask, 0.0)
    sig_l, val_l = sigmoid(mixed[:64]), mixed[64:128]
    sig_r, val_r = sigmoid(mixed[128:192]), mixed[192:]
    left = pack(sig_l * val_l * valid).astype(bf16)
    right = pack(sig_r * val_r * valid).astype(bf16)
    row, col = iota((128, 128), 0), iota((128, 128), 1)
    to_owner = one_hot(col == (row % 4) * 32 + (row // 8) * 2 + (row // 4) % 2)
    from_owner = one_hot(row == (col % 4) * 32 + (col // 8) * 2 + (col // 4) % 2)
    both = mul(to_owner, jnp.concatenate([left, right], axis=1), nn_dims)
    both = jnp.concatenate(
        [both[:, :128].reshape(n, 8, 128), both[:, 128:].reshape(n, 8, 128)], axis=1
    ).astype(bf16)
    s1[...] = both
    pl.semaphore_wait(barrier, n - 1)
    scatter(0, s1, r1, False)
    r1[me] = s1[me]

    wg = load("wg")[...]
    gating = sigmoid(mul(normed, wg, nn_dims)).astype(bf16).astype(f32)
    cot = load("cot")[...].reshape(cells, 128)
    wc_ref = load("wc")
    dact_ref[...] = mul(cot, wc_ref[...], nt_dims).astype(bf16)
    lane64 = iota((128, 64), 1)
    row64 = iota((128, 64), 0) // 4
    first = low_half(128)

    def spread(vector):
        low = jnp.sum(jnp.where(lane64 == row64, vector, 0.0), axis=1, keepdims=True)
        high = jnp.sum(jnp.where(lane64 == row64 + 32, vector, 0.0), axis=1, keepdims=True)
        return jnp.where(first, low, high).reshape(n, 8, 128)

    gain_e, shift_e = spread(load("gain_e")[...]), spread(load("shift_e")[...])
    gain2, shift2 = load("gain2")[...], load("shift2")[...]
    wo, wx_ref = load("wo")[...], load("wx")
    wxt_ref[...] = wx_ref[...].T
    by_pair = one_hot(col == ((row % 64) // 4) * 8 + (row // 64) * 4 + row % 4)
    pair_rows = one_hot(row == ((col % 64) // 4) * 8 + (col // 64) * 4 + col % 4)
    even = (iota((128, 128), 0) // 4) % 2 == 0

    arrive(0, r1)
    got = r1[...].astype(f32)
    left_all = got[:, :8].reshape(128, 128)
    right_all = mul(by_pair, got[:, 8:].reshape(128, 128).astype(bf16), nn_dims)
    first64 = low_half(64)

    def diagonal(x):
        return jnp.concatenate([jnp.where(first64, x, 0.0), jnp.where(first64, 0.0, x)], axis=0)

    diag0 = diagonal(right_all[:64]).astype(bf16)
    diag1 = diagonal(right_all[64:]).astype(bf16)

    def by_parity(x):
        return jnp.where(even, x, 0.0).astype(bf16), jnp.where(even, 0.0, x).astype(bf16)

    left0, left1 = by_parity(left_all)
    edges = mul(left0, diag0, nt_dims) + mul(left1, diag1, nt_dims)
    s2[...] = edges.reshape(n, 8, 128)
    scatter(1, s2, r2, False)
    r2[me] = s2[me]
    left_bf = left_all.astype(bf16)
    arrive(1, r2)

    edges_in = r2[...]
    inv_c = 1.0 / 64
    centred_e = edges_in - channel_sum(edges_in) * inv_c
    rstd_e = lax.rsqrt(channel_sum(centred_e * centred_e) * inv_c + epsilon)
    hat_e = centred_e * rstd_e
    edge_normed = (hat_e * gain_e + shift_e).reshape(128, 128).astype(bf16)
    edge_normed = unpack(mul(from_owner, edge_normed, nn_dims)).astype(bf16)
    update = mul(edge_normed, wo, tn_dims)
    middle = (state + gating * update).astype(bf16).astype(f32)
    centred2 = middle - jnp.mean(middle, axis=1, keepdims=True)
    rstd2 = lax.rsqrt(jnp.mean(centred2 * centred2, axis=1, keepdims=True) + epsilon)
    hat2 = centred2 * rstd2
    normed2 = (hat2 * gain2 + shift2).astype(bf16)
    units = wc_ref.shape[0]
    dnormed2 = jnp.zeros((cells, 128), f32)
    for begin in range(0, units, 256):
        w_swish = wx_ref[:, begin : begin + 256]
        w_linear = wx_ref[:, units + begin : units + begin + 256]
        swish_in = mul(normed2, w_swish, nn_dims)
        linear = mul(normed2, w_linear, nn_dims)
        dact = dact_ref[:, begin : begin + 256].astype(f32)
        sig = sigmoid(swish_in)
        silu = swish_in * sig
        dlinear = (dact * silu).astype(bf16)
        dswish = (dact * linear * (sig + silu * (1.0 - sig))).astype(bf16)
        swish_t = wxt_ref[begin : begin + 256]
        linear_t = wxt_ref[units + begin : units + begin + 256]
        dnormed2 = dnormed2 + mul(dswish, swish_t, nn_dims) + mul(dlinear, linear_t, nn_dims)
    dnormed2 = dnormed2.astype(bf16).astype(f32)
    dhat2 = dnormed2 * gain2
    dmiddle = rstd2 * (
        dhat2
        - jnp.mean(dhat2, axis=1, keepdims=True)
        - hat2 * jnp.mean(dhat2 * hat2, axis=1, keepdims=True)
    )
    late = (cot.astype(f32) + dmiddle).astype(bf16).astype(f32)
    dedge = mul(wo, (late * gating).astype(bf16), nt_dims)
    dedge = pack(dedge).astype(bf16)
    dedge = mul(to_owner, dedge, nn_dims).reshape(n, 8, 128)
    dhat_e = dedge * gain_e
    edge_raw = rstd_e * (
        dhat_e - channel_sum(dhat_e) * inv_c - hat_e * (channel_sum(dhat_e * hat_e) * inv_c)
    )
    s3[...] = edge_raw.astype(bf16).astype(f32)
    scatter(2, s3, r3, False)
    r3[me] = s3[me]

    gate_grad = (late * update).astype(bf16).astype(f32)
    dgate = (gate_grad * gating * (1.0 - gating)).astype(bf16)
    dnormed = mul(dgate, wg, nt_dims)
    gain2_sum = jnp.sum(dnormed2 * hat2, axis=0, keepdims=True)
    shift2_sum = jnp.sum(dnormed2, axis=0, keepdims=True)

    def collect(x):
        x = x.reshape(128, 128)
        low = jnp.sum(jnp.where(first, x, 0.0), axis=1, keepdims=True)
        high = jnp.sum(jnp.where(first, 0.0, x), axis=1, keepdims=True)
        spot = row // 4
        return jnp.sum(
            jnp.where(col == spot, low, 0.0) + jnp.where(col == spot + 32, high, 0.0),
            axis=0,
            keepdims=True,
        )

    gain_e_sum = collect(dedge * hat_e)
    shift_e_sum = collect(dedge)
    dsig_l = val_l * sig_l * (1.0 - sig_l) * valid
    dsig_r = val_r * sig_r * (1.0 - sig_r) * valid
    dval_l, dval_r = sig_l * valid, sig_r * valid

    arrive(2, r3)
    edge_round = r3[...].reshape(128, 128)
    round0, round1 = by_parity(edge_round)
    left_grad = mul(round0, diag0, nn_dims) + mul(round1, diag1, nn_dims)
    cross0 = mul(round0, left_bf, tn_dims)
    cross1 = mul(round1, left_bf, tn_dims)
    right_grad = jnp.concatenate(
        [
            jnp.where(first64, cross0[:64], cross0[64:]),
            jnp.where(first64, cross1[:64], cross1[64:]),
        ],
        axis=0,
    ).astype(bf16)
    right_grad = mul(pair_rows, right_grad, nn_dims)
    s4[...] = jnp.concatenate(
        [left_grad.reshape(n, 8, 128), right_grad.reshape(n, 8, 128)], axis=1
    ).astype(bf16)
    scatter(3, s4, r4, False)
    r4[me] = s4[me]
    arrive(3, r4)

    grads = r4[...].astype(f32)
    grads = jnp.concatenate(
        [grads[:, :8].reshape(128, 128), grads[:, 8:].reshape(128, 128)], axis=1
    ).astype(bf16)
    grads = mul(from_owner, grads, nn_dims)
    dleft, dright = unpack(grads[:, :128]), unpack(grads[:, 128:])
    dmixed = jnp.concatenate(
        [dleft * dsig_l, dleft * dval_l, dright * dsig_r, dright * dval_r], axis=0
    ).astype(bf16)
    dnormed = (dnormed + mul(dmixed, we_t, tn_dims)).astype(bf16).astype(f32)
    gain1_sum = jnp.sum(dnormed * hat1, axis=0, keepdims=True)
    shift1_sum = jnp.sum(dnormed, axis=0, keepdims=True)
    blank = jnp.zeros((2, 128), f32)
    s5[...] = jnp.concatenate(
        [gain1_sum, shift1_sum, gain2_sum, shift2_sum, gain_e_sum, shift_e_sum, blank], axis=0
    )
    scatter(4, s5, r5, True)
    r5[me] = s5[...]
    dhat1 = dnormed * gain1
    early = rstd1 * (
        dhat1
        - jnp.mean(dhat1, axis=1, keepdims=True)
        - hat1 * jnp.mean(dhat1 * hat1, axis=1, keepdims=True)
    )
    early = early.astype(bf16).astype(f32)
    out_ref[...] = (early + late).astype(bf16).reshape(out_ref.shape)
    arrive(4, r5)
    sums = jnp.sum(r5[...], axis=0) * (1.0 / tokens)
    norm_ref[...] = sums[:4]
    edge_ref[...] = sums[4:6, :64]
    for phase, buffer in enumerate((r1, r2, r3, r4, r5)):
        sent(phase, buffer)


def write_out(a, b, c, out_a, out_b, out_c, sem):
    copies = [
        pltpu.make_async_copy(source, target, sem.at[at])
        for at, (source, target) in enumerate(((a, out_a), (b, out_b), (c, out_c)))
    ]
    for copy in copies:
        copy.start()
    for copy in copies:
        copy.wait()


def fused_body(n, *args):
    (
        pair_state,
        cotangent,
        pair_mask,
        token_count,
        norm_gain,
        norm_shift,
        w_edges,
        w_gate,
        edge_gain,
        edge_shift,
        w_out,
        final_gain,
        final_shift,
        w_expand,
        w_contract,
    ) = args
    vmem = pl.BlockSpec(memory_space=pltpu.VMEM)
    operands = (
        pair_state,
        w_edges,
        norm_gain.reshape(1, -1),
        norm_shift.reshape(1, -1),
        pair_mask,
        token_count.reshape(1, 1),
        w_gate,
        cotangent,
        w_contract,
        edge_gain.reshape(1, -1),
        edge_shift.reshape(1, -1),
        w_out,
        final_gain.reshape(1, -1),
        final_shift.reshape(1, -1),
        w_expand,
    )
    cells = pair_state.shape[0] * pair_state.shape[1]
    tile = pltpu.VMEM((n, 8, 128), f32)
    pair = pltpu.VMEM((n, 16, 128), bf16)
    held = pl.pallas_call(
        functools.partial(fused_kernel, n),
        out_shape=(
            pltpu.VMEM(pair_state.shape, bf16),
            pltpu.VMEM((4, 128), f32),
            pltpu.VMEM((2, 64), f32),
        ),
        in_specs=[pl.BlockSpec(memory_space=pltpu.HBM)] * len(operands),
        out_specs=(vmem, vmem, vmem),
        scratch_shapes=[pltpu.VMEM(x.shape, x.dtype) for x in operands]
        + [
            pair,
            pair,
            tile,
            tile,
            tile,
            tile,
            pair,
            pair,
            pltpu.VMEM((8, 128), f32),
            tile,
            pltpu.VMEM((cells, w_contract.shape[0]), bf16),
            pltpu.VMEM(w_expand.shape[::-1], bf16),
            pltpu.SemaphoreType.DMA((5,)),
            pltpu.SemaphoreType.DMA((5,)),
            pltpu.SemaphoreType.DMA((len(operands),)),
        ],
        compiler_params=pltpu.CompilerParams(
            collective_id=0, has_side_effects=True, vmem_limit_bytes=60 * 1024 * 1024
        ),
    )(*operands)
    return pl.pallas_call(
        write_out,
        out_shape=tuple(jax.ShapeDtypeStruct(x.shape, x.dtype) for x in held),
        in_specs=[vmem] * 3,
        out_specs=(pl.BlockSpec(memory_space=pltpu.HBM),) * 3,
        scratch_shapes=[pltpu.SemaphoreType.DMA((3,))],
        compiler_params=pltpu.CompilerParams(vmem_limit_bytes=1024 * 1024),
    )(*held)


def pick_body(n):
    def chosen(*args):
        rows, tokens, _ = args[0].shape
        if (n, rows, tokens) == (16, 4, 64):
            return fused_body(n, *args)
        return body(*args)

    return chosen


def solution(mesh):
    in_specs = (
        P(("groups", "dap"), None, None),
        P(("groups", "dap"), None, None),
        P(("groups", "dap"), None),
        P("groups"),
        P(),
        P(),
        P(),
        P(),
        P(),
        P(),
        P(),
        P(),
        P(),
        P(),
        P(),
    )
    out_specs = (P(("groups", "dap"), None, None), P("groups", None), P("groups", None))
    chosen = pick_body(mesh.shape["dap"])
    return jax.shard_map(chosen, mesh=mesh, in_specs=in_specs, out_specs=out_specs, check_vma=False)
```
